512 devices in a mesh: dp: 32 (over z, x_hi, core), mp: 16 (over y, x_lo).
Axes of the slice: x: 4 (x_hi: 2, x_lo: 2; x = x_hi * 2 + x_lo), y: 8, z: 8, core: 2. Of those that a mesh axis runs over, the one named last changes fastest.
Arguments:
- points: bfloat16 [65536, 1024], P('dp', 'mp'), may hold values from -40 to 40
- point_cluster: int32 [65536, 1], P('dp'), may hold values from 0 to 12287, as said below
- cluster_parent: int32 [12288, 1], P(('dp', 'mp')), may hold values from 0 to 2047, as said below
Outputs:
- level2_centroids: bfloat16 [12288, 1024], P(('dp', 'mp'))
- level3_centroids: bfloat16 [2048, 1024], P('mp')
The draws below stay inside these ranges and needn't reach their ends.
Inputs may be any that keep to these rules, and one draw needn't show every extreme that they name: `point_cluster`: every level-2 centroid is named by at least one point; split the level-2 centroids into 512 aligned blocks of 24 consecutive ones: the 2048 points of one dp index name centroids of each block exactly 2048 / 512 times. `cluster_parent`: every level-3 centroid is named by at least one level-2 centroid.
All inputs are finite; a program needn't handle non-finite values.
Results may differ from the reference program's by a relative error of at most 0.0048.
Values may be sent and summed in bfloat16 or wider, within the bound.
No kernel may reach another device: no remote copies, remote signals or barrier semaphores. Data moves between devices by JAX's collectives and lax.ppermute only.
A program may use at most 64 MiB of HBM per device.

```python
import jax
import jax.numpy as jnp
from jax import lax

D = 1024
P_DEV = 2048
K2_MP = 768
NPTS = 65536
K2 = 12288
K3 = 2048
N_DP = 32
N_MP = 16


def spread_labels(key, count, limit):
    first, second, third, fourth = jax.random.split(key, 4)
    lower = jax.random.randint(first, (count,), 0, limit)
    upper = jax.random.randint(second, (count,), 0, limit)
    order = jax.random.permutation(third, limit)
    values = order[jnp.minimum(lower, upper)]
    spots = jax.random.permutation(fourth, count)[:limit]
    values = values.at[spots].set(jnp.arange(limit, dtype=jnp.int32))
    return values[:, None].astype(jnp.int32)


def draw_point_cluster(key, part):
    key = jax.random.fold_in(key, 7)
    first, second, third, fourth = jax.random.split(key, 4)
    block_rows = K2_MP // N_DP
    owners = N_DP * N_MP
    share = P_DEV // owners
    device_ids = jnp.arange(N_DP, dtype=jnp.int32)[:, None, None]
    copy_ids = jnp.arange(share, dtype=jnp.int32)[None, :, None]
    owner_ids = jnp.arange(owners, dtype=jnp.int32)[None, None, :]
    serial = device_ids * share + copy_ids
    lower = jax.random.randint(first, (N_DP, share, owners), 0, block_rows)
    upper = jax.random.randint(second, (N_DP, share, owners), 0, block_rows)
    offset = jax.random.randint(third, (owners,), 0, block_rows)
    skewed = (jnp.minimum(lower, upper) + offset[None, None, :]) % block_rows
    slots = jnp.where(serial < block_rows, serial + 0 * owner_ids, skewed)
    labels = (owner_ids * block_rows + slots).reshape(N_DP, share * owners).astype(jnp.int32)
    device_keys = jax.random.split(fourth, N_DP)
    labels = jax.vmap(jax.random.permutation)(device_keys, labels)
    return labels.reshape(NPTS, 1).astype(jnp.int32)


def draw_cluster_parent(key, part):
    key = jax.random.fold_in(key, 9)
    return spread_labels(key, K2, K3)


def draw_points(key, part):
    key = jax.random.fold_in(key, 5)
    first, second, third = jax.random.split(key, 3)
    column_scale = jnp.exp(jax.random.uniform(first, (D,), jnp.float32, -1.15, 1.15))
    row_scale = jnp.exp(jax.random.uniform(second, (NPTS, 1), jnp.float32, -1.15, 1.15))
    base = jnp.clip(jax.random.normal(third, (NPTS, D), jnp.float32), -5.0, 5.0)
    values = base * row_scale * column_scale * 0.5
    return values.astype(jnp.bfloat16)


def setup_inputs(seed: int = 0) -> dict:
    arg_keys = jax.random.split(jax.random.key(seed), 4)
    points = draw_points(jax.random.fold_in(arg_keys[3], 71), 0)
    point_cluster = draw_point_cluster(jax.random.fold_in(arg_keys[3], 71), 0)
    cluster_parent = draw_cluster_parent(jax.random.fold_in(arg_keys[3], 71), 0)
    return dict(points=points, point_cluster=point_cluster, cluster_parent=cluster_parent)


EPS = 1e-06

def unit_rows(total):
    return total * lax.rsqrt(lax.optimization_barrier(jnp.mean(total * total, axis=1, keepdims=True)) + EPS)

def reference(points, point_cluster, cluster_parent):
    labels = point_cluster[:, 0]
    sums = jax.ops.segment_sum(points.astype(jnp.float32), labels, num_segments=K2)
    counts = jax.ops.segment_sum(jnp.ones(labels.shape, jnp.float32), labels, num_segments=K2)
    level2 = unit_rows(sums).astype(jnp.bfloat16)
    weighted = counts[:, None] * level2.astype(jnp.float32)
    parents = jax.ops.segment_sum(weighted, cluster_parent[:, 0], num_segments=K3)
    level3 = unit_rows(parents).astype(jnp.bfloat16)
    return (level2, level3)
```

```python
import jax
import jax.numpy as jnp
from jax import lax
from jax.experimental import pallas as pl
from jax.experimental.pallas import tpu as pltpu
from jax.sharding import PartitionSpec as P

N_DP = 32
N_MP = 16
PTS = 2048
FEAT = 64
ROWS = 24
GROUP = ROWS * N_MP
D = 1024
K3 = 2048
K3_MP = 128
EPS = 1e-06

f32 = jnp.float32
bf16 = jnp.bfloat16
i32 = jnp.int32


def iota(shape, dim):
    return lax.broadcasted_iota(i32, shape, dim)


def hot(mask):
    return jnp.where(mask, 1.0, 0.0).astype(bf16)


def dot_nt(a, b):
    return lax.dot_general(a, b, (((1,), (1,)), ((), ())), preferred_element_type=f32)


def dot_nn(a, b):
    return lax.dot_general(a, b, (((1,), (0,)), ((), ())), preferred_element_type=f32)


def sort_kernel(labels_ref, points_ref, out_ref):
    labels = labels_ref[...]
    group = ((labels >> 7) * 171) >> 9
    local = labels - group * GROUP
    member = jnp.where(iota((N_DP, PTS), 0) == group, 1.0, 0.0)
    member16 = member.astype(bf16)
    width = 256
    n_chunks = PTS // width
    stacked = jnp.concatenate(
        [member16[:, c * width : (c + 1) * width] for c in range(n_chunks)], axis=0
    )
    before = hot(iota((width, 2 * width), 0) < iota((width, 2 * width), 1))
    prefix = dot_nn(stacked, before)
    base = jnp.zeros((N_DP, width), f32)
    ranks = []
    for c in range(n_chunks):
        part = prefix[c * N_DP : (c + 1) * N_DP]
        inside = member[:, c * width : (c + 1) * width]
        ranks.append(jnp.sum(inside * (part[:, :width] + base), axis=0, keepdims=True))
        base = base + part[:, width:]
    rank = jnp.concatenate(ranks, axis=1).astype(i32)
    r1 = rank & 3
    r2 = rank >> 2

    points = points_ref[...]
    split = jnp.concatenate([points * hot(r1 == r) for r in range(4)], axis=0)
    key = hot(iota((N_DP * 16, PTS), 0) == group * 16 + r2)
    moved = dot_nt(key, split)
    out_ref[:, 0:16, :] = moved[:, :128].reshape(N_DP, 16, 128).astype(bf16)
    out_ref[:, 16:32, :] = moved[:, 128:].reshape(N_DP, 16, 128).astype(bf16)

    side = r1 & 1
    high = (local >> 3).astype(f32)
    low = (local & 7).astype(f32)
    zero = jnp.zeros((4, PTS), f32)
    parts = jnp.concatenate(
        [
            jnp.where(side == 0, high, 0.0),
            jnp.where(side == 1, high, 0.0),
            jnp.where(side == 0, low, 0.0),
            jnp.where(side == 1, low, 0.0),
            zero,
        ],
        axis=0,
    )
    tagged = jnp.where(
        iota((N_DP, 8, PTS), 0) == group.reshape(1, 1, PTS), parts.reshape(1, 8, PTS), 0.0
    )
    place = hot(iota((128, PTS), 0) == (r1 >> 1) * 16 + r2)
    tags = dot_nt(tagged.reshape(N_DP * 8, PTS).astype(bf16), place)
    out_ref[:, 32:40, :] = tags.reshape(N_DP, 8, 128).astype(bf16)


def sum_kernel(in_ref, out_ref):
    data = in_ref[:, 0:32, :].reshape(N_DP * 32, 128)
    tags = in_ref[:, 32:40, :].astype(f32)
    sides = ([], [])
    for n in range(8):
        tile = tags[4 * n]
        for q in range(1, 4):
            tile = tile + pltpu.roll(tags[4 * n + q], 32 * q, 1)
        for s in range(2):
            sides[s].append(8.0 * tile[s : s + 1] + tile[2 + s : 3 + s])
    data = jnp.concatenate([data, jnp.ones((N_DP * 32, 128), bf16)], axis=1)
    totals = []
    for s in range(2):
        label = jnp.concatenate(sides[s], axis=1).astype(i32)
        totals.append(dot_nn(hot(iota((GROUP, N_DP * 32), 0) == label), data))
    lane = iota((GROUP, 128), 1)
    sums = jnp.where(lane < 64, totals[0][:, :128], totals[1][:, :128])
    sums = (sums + pltpu.roll(sums, 64, 1)).reshape(N_MP, 3, 8, 128)
    counts = (totals[0][:, 128:] + totals[1][:, 128:]).reshape(N_MP, 3, 8, 128)
    lane = iota((N_MP, 8, 128), 2)
    out_ref[:, 0:8, :] = jnp.where(lane < 64, sums[:, 0], sums[:, 1])
    tail = jnp.where(lane < 80, counts[:, 0], jnp.where(lane < 96, counts[:, 1], counts[:, 2]))
    out_ref[:, 8:16, :] = jnp.where(lane < 64, sums[:, 2], tail)


def unit_kernel(in_ref, parent_ref, level2_ref, out_ref):
    lane = iota((8, 128), 1)
    left = lane < 64
    rows = ([], [], [])
    for c in range(N_MP // 2):
        even, odd = in_ref[2 * c], in_ref[2 * c + 1]
        rows[0].append(jnp.where(left, even[:8], pltpu.roll(odd[:8], 64, 1)))
        rows[1].append(jnp.where(left, pltpu.roll(even[:8], 64, 1), odd[:8]))
        rows[2].append(jnp.where(left, even[8:], pltpu.roll(odd[8:], 64, 1)))
    tail = in_ref[0][8:]
    parent = parent_ref[...].astype(f32)
    level2 = []
    meta = jnp.zeros((8, 128), f32)
    for g in range(3):
        square = rows[g][0] * rows[g][0]
        for c in range(1, N_MP // 2):
            square = square + rows[g][c] * rows[g][c]
        scale = lax.rsqrt(jnp.sum(square, axis=1, keepdims=True) * (1.0 / D) + EPS)
        level2.append([(r * scale).astype(bf16).astype(f32) for r in rows[g]])
        pick = iota((8, ROWS), 1) == iota((8, ROWS), 0) + 8 * g
        mine = jnp.sum(jnp.where(pick, parent, 0.0), axis=1, keepdims=True).astype(i32)
        meta = jnp.where(lane == 96 + 4 * g, tail[:, 64 + 16 * g : 65 + 16 * g], meta)
        meta = jnp.where(lane == 97 + 4 * g, (mine >> 3).astype(f32), meta)
        meta = jnp.where(lane == 98 + 4 * g, (mine & 7).astype(f32), meta)
    level2_ref[...] = jnp.concatenate(
        [jnp.concatenate(level2[g], axis=1) for g in range(3)], axis=0
    ).astype(bf16)
    pieces = []
    for i in range(N_DP):
        c, b = divmod(i, 4)
        piece = meta
        for g in range(3):
            turned = level2[g][c]
            if g != b:
                turned = pltpu.roll(turned, (32 * (g - b)) % 128, 1)
            piece = jnp.where((lane >= 32 * g) & (lane < 32 * (g + 1)), turned, piece)
        pieces.append(piece.reshape(1, 8, 128))
    out_ref[...] = jnp.concatenate(pieces, axis=0).astype(bf16)


def parent_kernel(in_ref, out_ref):
    rows = N_DP * 8
    x = in_ref[...].astype(f32).reshape(rows, 128)
    lane = iota((rows, 128), 1)
    count = jnp.zeros((rows, 128), f32)
    for g in range(3):
        inside = (lane >= 32 * g) & (lane < 32 * (g + 1))
        count = jnp.where(inside, x[:, 96 + 4 * g : 97 + 4 * g], count)
    weighted = x * count
    high = weighted.astype(bf16).astype(f32)
    low = weighted - high
    high, low = high.T.astype(bf16), low.T.astype(bf16)
    total = jnp.zeros((64, K3), f32)
    for g in range(3):
        parent = (8.0 * x[:, 97 + 4 * g : 98 + 4 * g] + x[:, 98 + 4 * g : 99 + 4 * g]).astype(i32)
        chosen = hot(iota((rows, K3), 1) == parent)
        both = jnp.concatenate([high[32 * g : 32 * g + 32], low[32 * g : 32 * g + 32]], axis=0)
        total = total + dot_nn(both, chosen)
    total = total[:32] + total[32:]
    for j in range(N_MP):
        out_ref[j] = total[:, K3_MP * j : K3_MP * (j + 1)]


def spread_kernel(in_ref, out_ref):
    total = jnp.sum(in_ref[...], axis=0).astype(bf16)
    out_ref[...] = jnp.broadcast_to(total[None], (N_DP, 32, 128))


def finish_kernel(in_ref, out_ref):
    x = in_ref[...].astype(f32).reshape(D, 128)
    scale = lax.rsqrt(jnp.sum(x * x, axis=0, keepdims=True) * (1.0 / D) + EPS)
    y = x * scale
    for c in range(8):
        out_ref[:, 128 * c : 128 * (c + 1)] = y[128 * c : 128 * (c + 1)].T.astype(bf16)


def call(kernel, out, *args):
    vmem = pl.BlockSpec(memory_space=pltpu.VMEM)
    many = isinstance(out, tuple)
    return pl.pallas_call(
        kernel,
        out_shape=out,
        in_specs=[vmem] * len(args),
        out_specs=(vmem,) * len(out) if many else vmem,
        compiler_params=pltpu.CompilerParams(vmem_limit_bytes=48 * 1024 * 1024),
    )(*args)


def shape(dims, dtype):
    return jax.ShapeDtypeStruct(dims, dtype)


def exchange(x, axis):
    return lax.all_to_all(x, axis, 0, 0, tiled=True)


def body(points, point_cluster, cluster_parent):
    sent = call(sort_kernel, shape((N_DP, 40, 128), bf16), point_cluster.T, points.T)
    sums = call(sum_kernel, shape((N_MP, 16, 128), f32), exchange(sent, "dp"))
    level2, cut = call(
        unit_kernel,
        (shape((ROWS, D), bf16), shape((N_DP, 8, 128), bf16)),
        exchange(sums, "mp"),
        cluster_parent.T,
    )
    partial = call(parent_kernel, shape((N_MP, 32, 128), f32), exchange(cut, "dp"))
    parents = call(spread_kernel, shape((N_DP, 32, 128), bf16), exchange(partial, "mp"))
    level3 = call(finish_kernel, shape((K3_MP, D), bf16), exchange(parents, "dp"))
    return (level2, level3)


def solution(mesh):
    placed = (P("dp", "mp"), P("dp", None), P(("dp", "mp"), None))
    return jax.shard_map(
        body,
        mesh=mesh,
        in_specs=placed,
        out_specs=(P(("dp", "mp"), None), P("mp", None)),
        check_vma=False,
    )
```

```python
import jax
import jax.numpy as jnp
from jax import lax
from jax.experimental import pallas as pl
from jax.experimental.pallas import tpu as pltpu
from jax.sharding import PartitionSpec as P

N_DP = 32
N_MP = 16
PTS = 2048
FEAT = 64
ROWS = 24
GROUP = ROWS * N_MP
D = 1024
K3 = 2048
K3_MP = 128
EPS = 1e-06
STRIDE = 34

f32 = jnp.float32
bf16 = jnp.bfloat16
i32 = jnp.int32


def iota(shape, dim):
    return lax.broadcasted_iota(i32, shape, dim)


def hot(mask):
    return jnp.where(mask, 1.0, 0.0).astype(bf16)


def dot_nt(a, b):
    return lax.dot_general(a, b, (((1,), (1,)), ((), ())), preferred_element_type=f32)


def dot_nn(a, b):
    return lax.dot_general(a, b, (((1,), (0,)), ((), ())), preferred_element_type=f32)


def sort_kernel(labels_hbm, points_hbm, out_ref, labels_ref, points_ref, rows_ref, sems):
    fetch_labels = pltpu.make_async_copy(labels_hbm, labels_ref, sems.at[0])
    fetch_points = pltpu.make_async_copy(points_hbm, points_ref, sems.at[1])
    fetch_labels.start()
    fetch_points.start()
    fetch_labels.wait()
    labels = labels_ref[...]
    group = ((labels >> 7) * 171) >> 9
    local = labels - group * GROUP
    member = jnp.where(iota((N_DP, PTS), 0) == group, 1.0, 0.0)
    member16 = member.astype(bf16)
    width = 256
    n_chunks = PTS // width
    stacked = jnp.concatenate(
        [member16[:, c * width : (c + 1) * width] for c in range(n_chunks)], axis=0
    )
    before = hot(iota((width, 2 * width), 0) < iota((width, 2 * width), 1))
    prefix = dot_nn(stacked, before)
    base = jnp.zeros((N_DP, width), f32)
    ranks = []
    for c in range(n_chunks):
        part = prefix[c * N_DP : (c + 1) * N_DP]
        inside = member[:, c * width : (c + 1) * width]
        ranks.append(jnp.sum(inside * (part[:, :width] + base), axis=0, keepdims=True))
        base = base + part[:, width:]
    rank = jnp.concatenate(ranks, axis=1).astype(i32)
    r1 = rank & 3
    r2 = rank >> 2
    key = hot(iota((N_DP * 16, PTS), 0) == group * 16 + r2)

    line = iota((2 * N_DP, PTS), 0)
    digit = jnp.where((line & 1) == 0, local >> 3, local & 7).astype(f32)
    digit = jnp.where((line >> 1) == group, digit, 0.0).astype(bf16)
    turn = lax.axis_index("dp") * STRIDE
    spot = (turn + (r1 >> 1) * 16 + r2 + 64 * (r1 & 1)) & 127
    tags = dot_nt(digit, hot(iota((128, PTS), 0) == spot))

    fetch_points.wait()
    points = points_ref[...]
    split = jnp.concatenate([points * hot(r1 == r) for r in range(4)], axis=0)
    moved = dot_nt(key, split)
    for d in range(N_DP):
        rows_ref[STRIDE * d : STRIDE * d + 16, :] = moved[16 * d : 16 * d + 16, :128]
        rows_ref[STRIDE * d + 16 : STRIDE * d + 32, :] = moved[16 * d : 16 * d + 16, 128:]
        rows_ref[STRIDE * d + 32 : STRIDE * d + 34, :] = tags[2 * d : 2 * d + 2]
    out_ref[...] = rows_ref[...].astype(bf16)


def sum_kernel(parent_hbm, in_ref, out_ref, keep_ref, parent_ref, sem):
    fetch = pltpu.make_async_copy(parent_hbm, parent_ref, sem)
    fetch.start()
    total = N_DP * STRIDE
    data = in_ref[...]
    line, column = iota((N_DP, total), 0) * STRIDE, iota((N_DP, total), 1)
    weight = jnp.where(column == line + 32, 8.0, jnp.where(column == line + 33, 1.0, 0.0))
    tags = dot_nn(weight.astype(bf16), data)
    data = jnp.concatenate([data, jnp.ones((total, 128), bf16)], axis=1)
    results = []
    for s in range(2):
        if s == 1:
            tags = pltpu.roll(tags, 64, 1)
        tiles = []
        for t in range(-(-total // 128)):
            place = iota((N_DP, 128), 1) + 128 * t
            source = (place * 1928) >> 16
            tile = jnp.where(source == iota((N_DP, 128), 0), tags, 0.0)
            tile = jnp.sum(tile, axis=0, keepdims=True)
            tiles.append(jnp.where((place - source * STRIDE)[:1] < 32, tile, -1.0))
        label = jnp.concatenate(tiles, axis=1)[:, :total].astype(i32)
        results.append(dot_nn(hot(iota((GROUP, total), 0) == label), data))
    left = iota((GROUP, 128), 1) < 64
    sums = jnp.where(left, results[0][:, :128], results[1][:, :128])
    sums = sums + pltpu.roll(sums, 64, 1)
    counts = results[0][:, 128:] + results[1][:, 128:]
    turned = jnp.where(left, sums, counts).T
    keep_ref[...] = turned[:72]
    squares = jnp.sum(turned[:64] * turned[:64], axis=0, keepdims=True)
    squares = jnp.concatenate([squares[:, 128 * c : 128 * (c + 1)] for c in range(3)], axis=0)
    sums = sums.reshape(N_MP, 3, 8, 128)
    half = iota((N_MP, 8, 128), 2) < 64
    out_ref[:, 0:8, :] = jnp.where(half, sums[:, 0], sums[:, 1])
    last = sums[:, 2]
    out_ref[:, 8:12, :] = jnp.where(half[:, :4], last[:, :4], last[:, 4:])
    out_ref[:, 12:15, :] = jnp.broadcast_to(squares[None], (N_MP, 3, 128))
    fetch.wait()
    parent = parent_ref[...].astype(f32)
    parent = jnp.concatenate([parent, jnp.zeros((1, 128 - ROWS), f32)], axis=1)
    out_ref[:, 15:16, :] = jnp.broadcast_to(parent[None], (N_MP, 1, 128))


def unit_kernel(in_ref, keep_ref, level2_ref, out_ref):
    left = iota((8, 128), 1) < 64
    rows = ([], [], [])
    for c in range(N_MP // 2):
        even, odd = in_ref[2 * c], in_ref[2 * c + 1]
        turned_even, turned_odd = pltpu.roll(even, 64, 1), pltpu.roll(odd, 64, 1)
        rows[0].append(jnp.where(left, even[:8], turned_odd[:8]))
        rows[1].append(jnp.where(left, turned_even[:8], odd[:8]))
        upper = jnp.where(left, even[8:], turned_odd[8:])[:4]
        lower = jnp.where(left, turned_even[8:], odd[8:])[:4]
        rows[2].append(jnp.concatenate([upper, lower], axis=0))
    lines = jnp.concatenate([jnp.concatenate(r, axis=1) for r in rows], axis=0)
    scale = lax.rsqrt(jnp.sum(lines * lines, axis=1, keepdims=True) * (1.0 / D) + EPS)
    level2_ref[...] = (lines * scale).astype(bf16)

    squares = jnp.sum(in_ref[:, 8:16, :], axis=0)
    squares = jnp.concatenate([squares[4 + c : 5 + c] for c in range(3)], axis=1)
    scale = lax.rsqrt(squares * (1.0 / D) + EPS)
    named = jnp.concatenate(
        [pltpu.roll(in_ref[j, 15:16, :], (ROWS * j) % 128, 1) for j in range(N_MP)], axis=0
    )
    parent = []
    for c in range(3):
        place = iota((N_MP, 128), 1) + 128 * c
        mine = ((place >> 3) * 171) >> 9 == iota((N_MP, 128), 0)
        parent.append(jnp.sum(jnp.where(mine, named, 0.0), axis=0, keepdims=True))
    parent = jnp.concatenate(parent, axis=1).astype(i32)
    side = (parent >> 5) & 1
    device = (parent & 31) * N_MP + (parent >> 7)
    key = hot(iota((2 * N_DP * N_MP, GROUP), 0) == device * 2 + ((parent >> 6) & 1))

    weighted = (keep_ref[0:64, :] * scale).astype(bf16).astype(f32) * keep_ref[64:65, :]
    both = jnp.concatenate(
        [jnp.where(side == 0, weighted, 0.0), jnp.where(side == 1, weighted, 0.0)], axis=0
    )
    high = both.astype(bf16)
    low = (both - high.astype(f32)).astype(bf16)
    out_ref[...] = (dot_nt(key, high) + dot_nt(key, low)).astype(bf16)


def spread_kernel(in_ref, out_ref):
    total = jnp.sum(in_ref[...].astype(f32).reshape(N_DP, 32, 128), axis=0)
    left = iota((32, 128), 1) < 64
    above = pltpu.roll(total, 30, 0)
    first = jnp.where(left, total, pltpu.roll(above, 64, 1))
    second = jnp.where(left, pltpu.roll(total, 64, 1), above)
    rows = jnp.where((iota((32, 128), 0) & 3) < 2, first, pltpu.roll(second, 2, 0))
    square = jnp.sum((rows * rows).reshape(4, 8, 128), axis=0)
    square = jnp.sum(square + pltpu.roll(square, 4, 0), axis=1, keepdims=True)
    scale = lax.rsqrt(square * (1.0 / D) + EPS)
    rows = (rows.reshape(4, 8, 128) * scale[None]).reshape(32, 128)
    out_ref[...] = jnp.broadcast_to(rows.astype(bf16)[None], (N_DP, 32, 128))


def finish_kernel(in_ref, out_ref, rows_ref):
    rows_ref[...] = in_ref[...].astype(f32).reshape(N_DP * 32, 128)
    for c in range(8):
        for q, r in enumerate((0, 2, 1, 3)):
            out_ref[32 * r : 32 * (r + 1), 128 * c : 128 * (c + 1)] = rows_ref[
                pl.ds(4 * c + q, N_DP, stride=32), :
            ].astype(bf16)


def call(kernel, out, *args, far=(), scratch=()):
    vmem = pl.BlockSpec(memory_space=pltpu.VMEM)
    many = isinstance(out, tuple)
    return pl.pallas_call(
        kernel,
        out_shape=out,
        in_specs=[pl.BlockSpec(memory_space=pltpu.HBM)] * len(far) + [vmem] * len(args),
        out_specs=(vmem,) * len(out) if many else vmem,
        scratch_shapes=scratch,
        compiler_params=pltpu.CompilerParams(vmem_limit_bytes=48 * 1024 * 1024),
    )(*(pltpu.with_memory_space_constraint(x, pltpu.HBM) for x in far), *args)


def shape(dims, dtype):
    return jax.ShapeDtypeStruct(dims, dtype)


def exchange(x, axis):
    return lax.all_to_all(x, axis, 0, 0, tiled=True)


def body(points, point_cluster, cluster_parent):
    rows = N_DP * STRIDE
    sent = call(
        sort_kernel,
        shape((rows, 128), bf16),
        far=(point_cluster.T, points.T),
        scratch=(
            pltpu.VMEM((1, PTS), i32),
            pltpu.VMEM((FEAT, PTS), bf16),
            pltpu.VMEM((rows, 128), f32),
            pltpu.SemaphoreType.DMA((2,)),
        ),
    )
    got = exchange(sent.reshape(N_DP, STRIDE // 2, 2, 128), "dp").reshape(rows, 128)
    sums, keep = call(
        sum_kernel,
        (shape((N_MP, 16, 128), f32), shape((72, GROUP), f32)),
        got,
        far=(cluster_parent.T,),
        scratch=(pltpu.VMEM((1, ROWS), i32), pltpu.SemaphoreType.DMA(())),
    )
    devices = N_DP * N_MP
    level2, partial = call(
        unit_kernel,
        (shape((ROWS, D), bf16), shape((2 * devices, 128), bf16)),
        exchange(sums, "mp"),
        keep,
    )
    parts = exchange(partial.reshape(devices, 2, 128), ("dp", "mp")).reshape(2 * devices, 128)
    parents = call(spread_kernel, shape((N_DP, 32, 128), bf16), parts)
    level3 = call(
        finish_kernel,
        shape((K3_MP, D), bf16),
        exchange(parents, "dp"),
        scratch=(pltpu.VMEM((N_DP * 32, 128), f32),),
    )
    return (level2, level3)


def solution(mesh):
    placed = (P("dp", "mp"), P("dp", None), P(("dp", "mp"), None))
    return jax.shard_map(
        body,
        mesh=mesh,
        in_specs=placed,
        out_specs=(P(("dp", "mp"), None), P("mp", None)),
        check_vma=False,
    )
```

```python
import jax
import jax.numpy as jnp
from jax import lax
from jax.experimental import pallas as pl
from jax.experimental.pallas import tpu as pltpu
from jax.sharding import PartitionSpec as P

N_DP = 32
N_MP = 16
PTS = 2048
FEAT = 64
ROWS = 24
GROUP = ROWS * N_MP
D = 1024
K3 = 2048
K3_MP = 128
EPS = 1e-06
STRIDE = 34

f32 = jnp.float32
bf16 = jnp.bfloat16
i32 = jnp.int32


def iota(shape, dim):
    return lax.broadcasted_iota(i32, shape, dim)


def rows_of(row, n):
    one, zero = jnp.ones((), bf16), jnp.zeros((), bf16)
    blocks = []
    for at in range(0, n, 256):
        number = iota((min(256, n - at), row.shape[1]), 0).astype(f32).astype(bf16)
        blocks.append(jnp.where(number == (row - at).astype(bf16), one, zero))
    return jnp.concatenate(blocks, axis=0)


def hot(mask):
    return jnp.where(mask, 1.0, 0.0).astype(bf16)


def dot_nt(a, b):
    return lax.dot_general(a, b, (((1,), (1,)), ((), ())), preferred_element_type=f32)


def dot_nn(a, b):
    return lax.dot_general(a, b, (((1,), (0,)), ((), ())), preferred_element_type=f32)


def sort_kernel(labels_hbm, points_hbm, out_ref, labels_ref, points_ref, rows_ref, sems):
    fetch_labels = pltpu.make_async_copy(labels_hbm, labels_ref, sems.at[0])
    fetch_points = pltpu.make_async_copy(points_hbm, points_ref, sems.at[1])
    fetch_labels.start()
    fetch_points.start()
    fetch_labels.wait()
    labels = labels_ref[...]
    group = ((labels >> 7) * 171) >> 9
    local = labels - group * GROUP
    member = jnp.where(iota((N_DP, PTS), 0) == group, 1.0, 0.0)
    member16 = member.astype(bf16)
    width = 256
    n_chunks = PTS // width
    stacked = jnp.concatenate(
        [member16[:, c * width : (c + 1) * width] for c in range(n_chunks)], axis=0
    )
    before = hot(iota((width, 2 * width), 0) < iota((width, 2 * width), 1))
    prefix = dot_nn(stacked, before)
    base = jnp.zeros((N_DP, width), f32)
    ranks = []
    for c in range(n_chunks):
        part = prefix[c * N_DP : (c + 1) * N_DP]
        inside = member[:, c * width : (c + 1) * width]
        ranks.append(jnp.sum(inside * (part[:, :width] + base), axis=0, keepdims=True))
        base = base + part[:, width:]
    rank = jnp.concatenate(ranks, axis=1).astype(i32)
    r1 = rank & 7
    r2 = rank >> 3
    key = rows_of((group * 8 + r2).astype(f32), N_DP * 8)

    line = iota((2 * N_DP, PTS), 0)
    digit = jnp.where((line & 1) == 0, local >> 3, local & 7).astype(f32)
    digit = jnp.where((line >> 1) == group, digit, 0.0).astype(bf16)
    turn = lax.axis_index("dp") * STRIDE
    spot = (turn + (r1 >> 1) * 8 + r2 + 64 * (r1 & 1)) & 127
    tags = dot_nt(digit, rows_of(spot.astype(f32), 128))

    fetch_points.wait()
    points = points_ref[...]
    split = jnp.concatenate([points * hot(r1 == r) for r in range(8)], axis=0)
    moved = dot_nt(key, split)
    for d in range(N_DP):
        for h in range(4):
            at = STRIDE * d + 8 * h
            rows_ref[at : at + 8, :] = moved[8 * d : 8 * d + 8, 128 * h : 128 * (h + 1)]
        rows_ref[STRIDE * d + 32 : STRIDE * d + 34, :] = tags[2 * d : 2 * d + 2]
    out_ref[...] = rows_ref[...].astype(bf16)


def sum_kernel(parent_hbm, in_ref, out_ref, keep_ref, parent_ref, sem):
    fetch = pltpu.make_async_copy(parent_hbm, parent_ref, sem)
    fetch.start()
    total = N_DP * STRIDE
    data = in_ref[...]
    line, column = iota((N_DP, total), 0) * STRIDE, iota((N_DP, total), 1)
    weight = jnp.where(column == line + 32, 8.0, jnp.where(column == line + 33, 1.0, 0.0))
    tags = dot_nn(weight.astype(bf16), data)
    data = jnp.concatenate([data, jnp.ones((total, 128), bf16)], axis=1)
    results = []
    for s in range(2):
        if s == 1:
            tags = pltpu.roll(tags, 64, 1)
        tiles = []
        for t in range(-(-total // 128)):
            place = iota((N_DP, 128), 1) + 128 * t
            source = (place * 1928) >> 16
            tile = jnp.where(source == iota((N_DP, 128), 0), tags, 0.0)
            tile = jnp.sum(tile, axis=0, keepdims=True)
            tiles.append(jnp.where((place - source * STRIDE)[:1] < 32, tile, -1.0))
        label = jnp.concatenate(tiles, axis=1)[:, :total]
        results.append(dot_nn(rows_of(label, GROUP), data))
    left = iota((GROUP, 128), 1) < 64
    sums = jnp.where(left, results[0][:, :128], results[1][:, :128])
    sums = sums + pltpu.roll(sums, 64, 1)
    counts = results[0][:, 128:] + results[1][:, 128:]
    turned = jnp.where(left, sums, counts).T
    keep_ref[...] = turned[:72]
    squares = jnp.sum(turned[:64] * turned[:64], axis=0, keepdims=True)
    squares = jnp.concatenate([squares[:, 128 * c : 128 * (c + 1)] for c in range(3)], axis=0)
    sums = sums.reshape(N_MP, 3, 8, 128)
    half = iota((N_MP, 8, 128), 2) < 64
    out_ref[:, 0:8, :] = jnp.where(half, sums[:, 0], sums[:, 1])
    last = sums[:, 2]
    out_ref[:, 8:12, :] = jnp.where(half[:, :4], last[:, :4], last[:, 4:])
    out_ref[:, 12:15, :] = jnp.broadcast_to(squares[None], (N_MP, 3, 128))
    fetch.wait()
    parent = parent_ref[...].astype(f32)
    parent = jnp.concatenate([parent, jnp.zeros((1, 128 - ROWS), f32)], axis=1)
    out_ref[:, 15:16, :] = jnp.broadcast_to(parent[None], (N_MP, 1, 128))


def unit_kernel(in_ref, keep_ref, level2_ref, out_ref):
    left = iota((8, 128), 1) < 64
    rows = ([], [], [])
    for c in range(N_MP // 2):
        even, odd = in_ref[2 * c], in_ref[2 * c + 1]
        turned_even, turned_odd = pltpu.roll(even, 64, 1), pltpu.roll(odd, 64, 1)
        rows[0].append(jnp.where(left, even[:8], turned_odd[:8]))
        rows[1].append(jnp.where(left, turned_even[:8], odd[:8]))
        upper = jnp.where(left, even[8:], turned_odd[8:])[:4]
        lower = jnp.where(left, turned_even[8:], odd[8:])[:4]
        rows[2].append(jnp.concatenate([upper, lower], axis=0))
    lines = jnp.concatenate([jnp.concatenate(r, axis=1) for r in rows], axis=0)
    scale = lax.rsqrt(jnp.sum(lines * lines, axis=1, keepdims=True) * (1.0 / D) + EPS)
    level2_ref[...] = (lines * scale).astype(bf16)

    squares = jnp.sum(in_ref[:, 8:16, :], axis=0)
    squares = jnp.concatenate([squares[4 + c : 5 + c] for c in range(3)], axis=1)
    scale = lax.rsqrt(squares * (1.0 / D) + EPS)
    named = jnp.concatenate(
        [pltpu.roll(in_ref[j, 15:16, :], (ROWS * j) % 128, 1) for j in range(N_MP)], axis=0
    )
    parent = []
    for c in range(3):
        place = iota((N_MP, 128), 1) + 128 * c
        mine = ((place >> 3) * 171) >> 9 == iota((N_MP, 128), 0)
        parent.append(jnp.sum(jnp.where(mine, named, 0.0), axis=0, keepdims=True))
    parent = jnp.concatenate(parent, axis=1).astype(i32)
    side = (parent >> 5) & 1
    device = (parent & 31) * N_MP + (parent >> 7)
    key = rows_of((device * 2 + ((parent >> 6) & 1)).astype(f32), 2 * N_DP * N_MP)

    weighted = (keep_ref[0:64, :] * scale).astype(bf16).astype(f32) * keep_ref[64:65, :]
    both = jnp.concatenate(
        [jnp.where(side == 0, weighted, 0.0), jnp.where(side == 1, weighted, 0.0)], axis=0
    )
    high = both.astype(bf16)
    low = (both - high.astype(f32)).astype(bf16)
    total = dot_nt(key, jnp.concatenate([high, low], axis=0))
    out_ref[...] = (total[:, :128] + total[:, 128:]).astype(bf16)


def spread_kernel(in_ref, out_ref):
    total = jnp.sum(in_ref[...].astype(f32).reshape(N_DP, 32, 128), axis=0)
    left = iota((32, 128), 1) < 64
    above = pltpu.roll(total, 30, 0)
    first = jnp.where(left, total, pltpu.roll(above, 64, 1))
    second = jnp.where(left, pltpu.roll(total, 64, 1), above)
    rows = jnp.where((iota((32, 128), 0) & 3) < 2, first, pltpu.roll(second, 2, 0))
    square = jnp.sum((rows * rows).reshape(4, 8, 128), axis=0)
    square = jnp.sum(square + pltpu.roll(square, 4, 0), axis=1, keepdims=True)
    scale = lax.rsqrt(square * (1.0 / D) + EPS)
    rows = (rows.reshape(4, 8, 128) * scale[None]).reshape(32, 128)
    out_ref[...] = jnp.broadcast_to(rows.astype(bf16)[None], (N_DP, 32, 128))


def finish_kernel(in_ref, out_ref, rows_ref):
    for i in range(N_DP):
        rows_ref[33 * i : 33 * i + 32, :] = in_ref[i].astype(f32)
    for c in range(8):
        for q, r in enumerate((0, 2, 1, 3)):
            out_ref[32 * r : 32 * (r + 1), 128 * c : 128 * (c + 1)] = rows_ref[
                pl.ds(4 * c + q, N_DP, stride=33), :
            ].astype(bf16)


def call(kernel, out, *args, far=(), scratch=()):
    vmem = pl.BlockSpec(memory_space=pltpu.VMEM)
    many = isinstance(out, tuple)
    return pl.pallas_call(
        kernel,
        out_shape=out,
        in_specs=[pl.BlockSpec(memory_space=pltpu.HBM)] * len(far) + [vmem] * len(args),
        out_specs=(vmem,) * len(out) if many else vmem,
        scratch_shapes=scratch,
        compiler_params=pltpu.CompilerParams(vmem_limit_bytes=48 * 1024 * 1024),
    )(*(pltpu.with_memory_space_constraint(x, pltpu.HBM) for x in far), *args)


def shape(dims, dtype):
    return jax.ShapeDtypeStruct(dims, dtype)


def exchange(x, axis):
    return lax.all_to_all(x, axis, 0, 0, tiled=True)


def body(points, point_cluster, cluster_parent):
    rows = N_DP * STRIDE
    sent = call(
        sort_kernel,
        shape((rows, 128), bf16),
        far=(point_cluster.T, points.T),
        scratch=(
            pltpu.VMEM((1, PTS), i32),
            pltpu.VMEM((FEAT, PTS), bf16),
            pltpu.VMEM((rows, 128), f32),
            pltpu.SemaphoreType.DMA((2,)),
        ),
    )
    got = exchange(sent.reshape(N_DP, STRIDE // 2, 2, 128), "dp").reshape(rows, 128)
    sums, keep = call(
        sum_kernel,
        (shape((N_MP, 16, 128), f32), shape((72, GROUP), f32)),
        got,
        far=(cluster_parent.T,),
        scratch=(pltpu.VMEM((1, ROWS), i32), pltpu.SemaphoreType.DMA(())),
    )
    devices = N_DP * N_MP
    level2, partial = call(
        unit_kernel,
        (shape((ROWS, D), bf16), shape((2 * devices, 128), bf16)),
        exchange(sums, "mp"),
        keep,
    )
    parts = exchange(partial.reshape(devices, 2, 128), ("dp", "mp")).reshape(2 * devices, 128)
    parents = call(spread_kernel, shape((N_DP, 32, 128), bf16), parts)
    level3 = call(
        finish_kernel,
        shape((K3_MP, D), bf16),
        exchange(parents, "dp"),
        scratch=(pltpu.VMEM((N_DP * 33, 128), f32),),
    )
    return (level2, level3)


def solution(mesh):
    placed = (P("dp", "mp"), P("dp", None), P(("dp", "mp"), None))
    return jax.shard_map(
        body,
        mesh=mesh,
        in_specs=placed,
        out_specs=(P(("dp", "mp"), None), P("mp", None)),
        check_vma=False,
    )
```

```python
import jax
import jax.numpy as jnp
from jax import lax
from jax.experimental import pallas as pl
from jax.experimental.pallas import tpu as pltpu
from jax.sharding import Mesh
from jax.sharding import PartitionSpec as P

N_DP = 32
N_MP = 16
PTS = 2048
FEAT = 64
ROWS = 24
GROUP = ROWS * N_MP
D = 1024
K3 = 2048
K3_MP = 128
EPS = 1e-06
STRIDE = 34

f32 = jnp.float32
bf16 = jnp.bfloat16
i32 = jnp.int32


def iota(shape, dim):
    return lax.broadcasted_iota(i32, shape, dim)


def rows_of(row, n):
    one, zero = jnp.ones((), bf16), jnp.zeros((), bf16)
    blocks = []
    for at in range(0, n, 256):
        number = iota((min(256, n - at), row.shape[1]), 0).astype(f32).astype(bf16)
        blocks.append(jnp.where(number == (row - at).astype(bf16), one, zero))
    return jnp.concatenate(blocks, axis=0)


def hot(mask):
    return jnp.where(mask, 1.0, 0.0).astype(bf16)


def dot_nt(a, b):
    return lax.dot_general(a, b, (((1,), (1,)), ((), ())), preferred_element_type=f32)


def dot_nn(a, b):
    return lax.dot_general(a, b, (((1,), (0,)), ((), ())), preferred_element_type=f32)


def sort_kernel(labels_hbm, points_hbm, out_ref, labels_ref, points_ref, rows_ref, sems):
    fetch_labels = pltpu.make_async_copy(labels_hbm, labels_ref, sems.at[0])
    fetch_points = pltpu.make_async_copy(points_hbm, points_ref, sems.at[1])
    fetch_labels.start()
    fetch_points.start()
    fetch_labels.wait()
    labels = labels_ref[...]
    group = ((labels >> 7) * 171) >> 9
    local = labels - group * GROUP
    member = jnp.where(iota((N_DP, PTS), 0) == group, 1.0, 0.0)
    member16 = member.astype(bf16)
    width = 256
    n_chunks = PTS // width
    stacked = jnp.concatenate(
        [member16[:, c * width : (c + 1) * width] for c in range(n_chunks)], axis=0
    )
    before = hot(iota((width, 2 * width), 0) < iota((width, 2 * width), 1))
    prefix = dot_nn(stacked, before)
    base = jnp.zeros((N_DP, width), f32)
    ranks = []
    for c in range(n_chunks):
        part = prefix[c * N_DP : (c + 1) * N_DP]
        inside = member[:, c * width : (c + 1) * width]
        ranks.append(jnp.sum(inside * (part[:, :width] + base), axis=0, keepdims=True))
        base = base + part[:, width:]
    rank = jnp.concatenate(ranks, axis=1).astype(i32)
    r1 = rank & 7
    r2 = rank >> 3
    key = rows_of((group * 8 + r2).astype(f32), N_DP * 8)

    line = iota((2 * N_DP, PTS), 0)
    digit = jnp.where((line & 1) == 0, local >> 3, local & 7).astype(f32)
    digit = jnp.where((line >> 2) == (group >> 1), digit, 0.0).astype(bf16)
    place = lax.axis_index("pair") * 2 + lax.axis_index("core")
    slot = (group & 1) * 4 + (r1 & 3)
    spot = (16 * (place + slot) + (r1 >> 2) * 8 + r2) & 127
    tags = dot_nt(digit, rows_of(spot.astype(f32), 128))

    fetch_points.wait()
    points = points_ref[...]
    masks = [hot(r1 == r) for r in range(8)]
    split = jnp.concatenate(
        [points[32 * half : 32 * half + 32] * masks[r] for half in range(2) for r in range(8)], axis=0
    )
    moved = dot_nt(key, split)
    for d in range(N_DP):
        pair, half = d >> 1, d & 1
        for own in range(2):
            for h in range(2):
                at = STRIDE * d + 16 * own + 8 * h
                line, lane = 8 * (2 * pair + own), 256 * half + 128 * h
                rows_ref[at : at + 8, :] = moved[line : line + 8, lane : lane + 128]
        rows_ref[STRIDE * d + 32 : STRIDE * d + 34, :] = tags[2 * d : 2 * d + 2]
    out_ref[...] = rows_ref[...].astype(bf16)


def sum_kernel(parent_hbm, in_ref, out_ref, keep_ref, parent_ref, rows_ref, sem):
    fetch = pltpu.make_async_copy(parent_hbm, parent_ref, sem)
    fetch.start()
    rows_ref[...] = in_ref[...].astype(f32)
    tags = 8.0 * rows_ref[pl.ds(32, N_DP, stride=STRIDE), :] + rows_ref[pl.ds(33, N_DP, stride=STRIDE), :]
    mine = iota((8, 128), 1) >> 4 == iota((8, 128), 0)
    quarter = iota((GROUP, 128), 1) >> 5
    half = N_DP * 16
    halves, squares = [], []
    for own in range(2):
        data = jnp.concatenate(
            [rows_ref[STRIDE * i + 16 * own : STRIDE * i + 16 * own + 16, :] for i in range(N_DP)], axis=0
        ).astype(bf16)
        data = jnp.concatenate([data, jnp.ones((half, 128), bf16)], axis=1)
        sums, counts = jnp.zeros((GROUP, 128), f32), jnp.zeros((GROUP, 128), f32)
        for s in range(4):
            slot = own * 4 + s
            turned = pltpu.roll(tags, 128 - 16 * slot, 1) if slot else tags
            label = jnp.concatenate(
                [
                    jnp.sum(jnp.where(mine, turned[8 * t : 8 * t + 8], 0.0), axis=0, keepdims=True)
                    for t in range(4)
                ],
                axis=1,
            )
            result = dot_nn(rows_of(label, GROUP), data)
            sums = jnp.where(quarter == s, result[:, :128], sums)
            counts = counts + result[:, 128:]
        sums = sums + pltpu.roll(sums, 64, 1)
        sums = sums + pltpu.roll(sums, 32, 1)
        turned = jnp.where(quarter == 0, sums, counts).T
        keep_ref[:, own * GROUP : (own + 1) * GROUP] = turned[:40]
        square = jnp.sum(turned[:32] * turned[:32], axis=0, keepdims=True)
        squares += [square[:, 128 * c : 128 * (c + 1)] for c in range(3)]
        sums = sums.reshape(N_MP, 3, 8, 128)
        band = iota((N_MP, 8, 128), 2) >> 5
        wide = jnp.where(band == 0, sums[:, 0], jnp.where(band == 1, sums[:, 1], sums[:, 2]))
        high = wide.astype(bf16)
        halves.append((high, (wide - high.astype(f32)).astype(bf16)))
    fetch.wait()
    parent = parent_ref[...]
    parent = jnp.concatenate([parent >> 3, parent & 7], axis=0).astype(f32)
    parent = jnp.concatenate([parent, jnp.zeros((2, 128 - ROWS), f32)], axis=1)
    tail = jnp.concatenate(squares + [parent], axis=0).astype(bf16)
    for own in range(2):
        block = slice(N_MP * own, N_MP * (own + 1))
        out_ref[block, 0:8, :] = halves[own][0]
        out_ref[block, 8:16, :] = halves[own][1]
    out_ref[:, 16:24, :] = jnp.broadcast_to(tail[None], (2 * N_MP, 8, 128))


def unit_kernel(in_ref, keep_ref, level2_ref, out_ref):
    band = iota((8, 128), 1) >> 5
    rows = ([], [], [])
    for c in range(N_MP // 2):
        parts = []
        for b in range(4):
            source = N_MP * (b & 1) + 2 * c + (b >> 1)
            parts.append(in_ref[source, 0:8, :].astype(f32) + in_ref[source, 8:16, :].astype(f32))
        for g in range(3):
            line = None
            for b in range(4):
                part = pltpu.roll(parts[b], (32 * (b - g)) % 128, 1) if b != g else parts[b]
                line = part if line is None else jnp.where(band == b, part, line)
            rows[g].append(line)
    lines = jnp.concatenate([jnp.concatenate(r, axis=1) for r in rows], axis=0)
    scale = lax.rsqrt(jnp.sum(lines * lines, axis=1, keepdims=True) * (1.0 / D) + EPS)
    level2_ref[...] = (lines * scale).astype(bf16)

    tails = in_ref[:, 16:24, :].astype(f32)
    squares = jnp.sum(tails, axis=0)
    squares = jnp.concatenate([squares[c : c + 1] for c in range(6)], axis=1)
    scale = lax.rsqrt(squares * (1.0 / D) + EPS)
    named = 8.0 * tails[:, 6:7] + tails[:, 7:8]
    named = jnp.concatenate(
        [pltpu.roll(named[n], (ROWS * n) % 128, 1) if n % N_MP else named[n] for n in range(2 * N_MP)], axis=0
    )
    parent = []
    for c in range(6):
        place = iota((2 * N_MP, 128), 1) + 128 * c
        mine = ((place >> 3) * 171) >> 9 == iota((2 * N_MP, 128), 0)
        parent.append(jnp.sum(jnp.where(mine, named, 0.0), axis=0, keepdims=True))
    parent = jnp.concatenate(parent, axis=1).astype(i32)
    device = ((parent >> 3) & 15) * N_MP + (parent >> 7)
    key = rows_of((device * 2 + (parent & 1)).astype(f32), N_DP * N_MP)

    weighted = (keep_ref[0:32, :] * scale).astype(bf16).astype(f32) * keep_ref[32:33, :]
    part = (parent >> 1) & 3
    both = jnp.concatenate([jnp.where(part == s, weighted, 0.0) for s in range(4)], axis=0)
    high = both.astype(bf16)
    low = (both - high.astype(f32)).astype(bf16)
    total = dot_nt(key, jnp.concatenate([high, low], axis=0))
    out_ref[...] = (total[:, :128] + total[:, 128:]).astype(bf16)


def spread_kernel(in_ref, out_ref):
    total = jnp.sum(in_ref[...].astype(f32).reshape(N_MP, 32, 128), axis=0).reshape(4, 8, 128)
    band, part = iota((4, 8, 128), 2) >> 5, iota((4, 8, 128), 1) >> 1
    turned = [total] + [pltpu.roll(total, 32 * d, 2) for d in range(1, 4)]
    out = jnp.zeros((4, 8, 128), f32)
    for b, j in enumerate((0, 2, 1, 3)):
        for s in range(4):
            piece = turned[(b - s) % 4]
            if s != j:
                piece = pltpu.roll(piece, (2 * (s - j)) % 8, 1)
            out = jnp.where((band == b) & (part == s), piece, out)
    out = jnp.where(lax.axis_index("core") == 1, pltpu.roll(out, 32, 2), out)
    out_ref[...] = jnp.broadcast_to(out.reshape(32, 128).astype(bf16)[None], (N_DP, 32, 128))


def finish_kernel(in_ref, out_ref):
    band = iota((N_MP, 8, 128), 2) >> 5
    tiles = []
    square = jnp.zeros((N_MP, 8, 128), f32)
    for t in range(4):
        block = pl.ds(8 * t, 8)
        first = jnp.concatenate([in_ref[2 * p : 2 * p + 1, block, :] for p in range(N_MP)], axis=0).astype(f32)
        second = jnp.concatenate([in_ref[2 * p + 1 : 2 * p + 2, block, :] for p in range(N_MP)], axis=0).astype(f32)
        even = (band & 1) == 0
        tiles.append(jnp.where(even, first, second))
        tiles.append(pltpu.roll(jnp.where(even, second, first), 96, 2))
        square = square + tiles[-1] * tiles[-1] + tiles[-2] * tiles[-2]
    scale = lax.rsqrt(jnp.sum(square, axis=2, keepdims=True) * (1.0 / D) + EPS)
    for c in range(8):
        out_ref[:, 128 * c : 128 * (c + 1)] = (tiles[c] * scale).reshape(K3_MP, 128).astype(bf16)


def call(kernel, out, *args, far=(), scratch=()):
    vmem = pl.BlockSpec(memory_space=pltpu.VMEM)
    many = isinstance(out, tuple)
    return pl.pallas_call(
        kernel,
        out_shape=out,
        in_specs=[pl.BlockSpec(memory_space=pltpu.HBM)] * len(far) + [vmem] * len(args),
        out_specs=(vmem,) * len(out) if many else vmem,
        scratch_shapes=scratch,
        compiler_params=pltpu.CompilerParams(vmem_limit_bytes=48 * 1024 * 1024),
    )(*(pltpu.with_memory_space_constraint(x, pltpu.HBM) for x in far), *args)


def shape(dims, dtype):
    return jax.ShapeDtypeStruct(dims, dtype)


def exchange(x, axis):
    return lax.all_to_all(x, axis, 0, 0, tiled=True)


def body(points, point_cluster, cluster_parent):
    rows = N_DP * STRIDE
    sent = call(
        sort_kernel,
        shape((rows, 128), bf16),
        far=(point_cluster.T, points.T),
        scratch=(
            pltpu.VMEM((1, PTS), i32),
            pltpu.VMEM((FEAT, PTS), bf16),
            pltpu.VMEM((rows, 128), f32),
            pltpu.SemaphoreType.DMA((2,)),
        ),
    )
    got = exchange(sent.reshape(N_DP, STRIDE // 2, 2, 128), ("pair", "core")).reshape(rows, 128)
    sums, keep = call(
        sum_kernel,
        (shape((2 * N_MP, 24, 128), bf16), shape((40, 2 * GROUP), f32)),
        got,
        far=(cluster_parent.T,),
        scratch=(
            pltpu.VMEM((1, ROWS), i32),
            pltpu.VMEM((rows, 128), f32),
            pltpu.SemaphoreType.DMA(()),
        ),
    )
    peers = N_DP // 2 * N_MP
    level2, partial = call(
        unit_kernel,
        (shape((ROWS, D), bf16), shape((2 * peers, 128), bf16)),
        exchange(sums, ("core", "mp")),
        keep,
    )
    parts = exchange(partial.reshape(peers, 2, 128), ("pair", "mp")).reshape(2 * peers, 128)
    parents = call(spread_kernel, shape((N_DP, 32, 128), bf16), parts)
    level3 = call(finish_kernel, shape((K3_MP, D), bf16), exchange(parents, ("pair", "core")))
    return (level2, level3)


def solution(mesh):
    pairs = Mesh(mesh.devices.reshape(N_DP // 2, 2, N_MP), ("pair", "core", "mp"))
    dp = ("pair", "core")
    placed = (P(dp, "mp"), P(dp, None), P((*dp, "mp"), None))
    return jax.shard_map(
        body,
        mesh=pairs,
        in_specs=placed,
        out_specs=(P((*dp, "mp"), None), P("mp", None)),
        check_vma=False,
    )
```

```python
import jax
import jax.numpy as jnp
from jax import lax
from jax.experimental import pallas as pl
from jax.experimental.pallas import tpu as pltpu
from jax.sharding import Mesh
from jax.sharding import PartitionSpec as P

N_DP = 32
N_MP = 16
PTS = 2048
FEAT = 64
ROWS = 24
GROUP = ROWS * N_MP
D = 1024
K3 = 2048
K3_MP = 128
EPS = 1e-06
STRIDE = 34

f32 = jnp.float32
bf16 = jnp.bfloat16
i32 = jnp.int32


def iota(shape, dim):
    return lax.broadcasted_iota(i32, shape, dim)


def rows_of(row, n):
    one, zero = jnp.ones((), bf16), jnp.zeros((), bf16)
    blocks = []
    for at in range(0, n, 256):
        number = iota((min(256, n - at), row.shape[1]), 0).astype(f32).astype(bf16)
        blocks.append(jnp.where(number == (row - at).astype(bf16), one, zero))
    return jnp.concatenate(blocks, axis=0)


def hot(mask):
    return jnp.where(mask, 1.0, 0.0).astype(bf16)


def dot_nt(a, b):
    return lax.dot_general(a, b, (((1,), (1,)), ((), ())), preferred_element_type=f32)


def dot_nn(a, b):
    return lax.dot_general(a, b, (((1,), (0,)), ((), ())), preferred_element_type=f32)


def sort_kernel(labels_hbm, points_hbm, out_ref, labels_ref, points_ref, rows_ref, sems):
    fetch_labels = pltpu.make_async_copy(labels_hbm, labels_ref, sems.at[0])
    fetch_points = pltpu.make_async_copy(points_hbm, points_ref, sems.at[1])
    fetch_labels.start()
    fetch_points.start()
    fetch_labels.wait()
    labels = labels_ref[...]
    group = ((labels >> 7) * 171) >> 9
    local = labels - group * GROUP
    member = jnp.where(iota((N_DP, PTS), 0) == group, 1.0, 0.0)
    member16 = member.astype(bf16)
    width = 256
    n_chunks = PTS // width
    stacked = jnp.concatenate(
        [member16[:, c * width : (c + 1) * width] for c in range(n_chunks)], axis=0
    )
    before = hot(iota((width, 2 * width), 0) < iota((width, 2 * width), 1))
    prefix = dot_nn(stacked, before)
    base = jnp.zeros((N_DP, width), f32)
    ranks = []
    for c in range(n_chunks):
        part = prefix[c * N_DP : (c + 1) * N_DP]
        inside = member[:, c * width : (c + 1) * width]
        ranks.append(jnp.sum(inside * (part[:, :width] + base), axis=0, keepdims=True))
        base = base + part[:, width:]
    rank = jnp.concatenate(ranks, axis=1).astype(i32)
    r1 = rank & 7
    r2 = rank >> 3
    key = rows_of((group * 8 + r2).astype(f32), N_DP * 8)

    line = iota((2 * N_DP, PTS), 0)
    digit = jnp.where((line & 1) == 0, local >> 3, local & 7).astype(f32)
    digit = jnp.where((line >> 2) == (group >> 1), digit, 0.0).astype(bf16)
    place = lax.axis_index("pair") * 2 + lax.axis_index("core")
    slot = (group & 1) * 4 + (r1 & 3)
    spot = (16 * (place + slot) + (r1 >> 2) * 8 + r2) & 127
    tags = dot_nt(digit, rows_of(spot.astype(f32), 128))

    fetch_points.wait()
    points = points_ref[...]
    masks = [hot(r1 == r) for r in range(8)]
    split = jnp.concatenate(
        [points[32 * half : 32 * half + 32] * masks[r] for half in range(2) for r in range(8)], axis=0
    )
    moved = dot_nt(key, split)
    for d in range(N_DP):
        pair, half = d >> 1, d & 1
        for own in range(2):
            for h in range(2):
                at = STRIDE * d + 16 * own + 8 * h
                line, lane = 8 * (2 * pair + own), 256 * half + 128 * h
                rows_ref[at : at + 8, :] = moved[line : line + 8, lane : lane + 128]
        rows_ref[STRIDE * d + 32 : STRIDE * d + 34, :] = tags[2 * d : 2 * d + 2]
    out_ref[...] = rows_ref[...].astype(bf16)


def sum_kernel(parent_hbm, in_ref, out_ref, keep_ref, parent_ref, rows_ref, sem):
    fetch = pltpu.make_async_copy(parent_hbm, parent_ref, sem)
    fetch.start()
    rows_ref[...] = in_ref[...].astype(f32)
    tags = 8.0 * rows_ref[pl.ds(32, N_DP, stride=STRIDE), :] + rows_ref[pl.ds(33, N_DP, stride=STRIDE), :]
    mine = iota((8, 128), 1) >> 4 == iota((8, 128), 0)
    quarter = iota((GROUP, 128), 1) >> 5
    half = N_DP * 16
    sides = [hot(iota((1, 128), 1) >> 5 == s) for s in range(4)]
    wides, squares = [], []
    for own in range(2):
        data = jnp.concatenate(
            [rows_ref[STRIDE * i + 16 * own : STRIDE * i + 16 * own + 16, :] for i in range(N_DP)], axis=0
        ).astype(bf16)
        labels = []
        for s in range(4):
            slot = own * 4 + s
            turned = pltpu.roll(tags, 128 - 16 * slot, 1) if slot else tags
            labels += [
                jnp.sum(jnp.where(mine, turned[8 * t : 8 * t + 8], 0.0), axis=0, keepdims=True)
                for t in range(4)
            ]
        split = jnp.concatenate([data * side for side in sides], axis=0)
        split = jnp.concatenate([split, jnp.ones((4 * half, 128), bf16)], axis=1)
        result = dot_nn(rows_of(jnp.concatenate(labels, axis=1), GROUP), split)
        sums, counts = result[:, :128], result[:, 128:]
        sums = sums + pltpu.roll(sums, 64, 1)
        sums = sums + pltpu.roll(sums, 32, 1)
        turned = jnp.where(quarter == 0, sums, counts).T
        keep_ref[:, own * GROUP : (own + 1) * GROUP] = turned[:40]
        square = jnp.sum(turned[:32] * turned[:32], axis=0, keepdims=True)
        squares += [square[:, 128 * c : 128 * (c + 1)] for c in range(3)]
        sums = sums.reshape(N_MP, 3, 8, 128)
        band = iota((N_MP, 8, 128), 2) >> 5
        wide = jnp.where(band == 0, sums[:, 0], jnp.where(band == 1, sums[:, 1], sums[:, 2]))
        wides.append(wide.astype(bf16))
    fetch.wait()
    parent = parent_ref[...]
    parent = jnp.concatenate([parent >> 3, parent & 7], axis=0).astype(f32)
    parent = jnp.concatenate([parent, jnp.zeros((2, 128 - ROWS), f32)], axis=1)
    tail = jnp.concatenate(squares + [parent], axis=0).astype(bf16)
    for own in range(2):
        block = slice(N_MP * own, N_MP * (own + 1))
        out_ref[block, 0:8, :] = wides[own]
    out_ref[:, 8:16, :] = jnp.broadcast_to(tail[None], (2 * N_MP, 8, 128))


def unit_kernel(in_ref, keep_ref, level2_ref, out_ref):
    band = iota((8, 128), 1) >> 5
    rows = ([], [], [])
    for c in range(N_MP // 2):
        parts = []
        for b in range(4):
            source = N_MP * (b & 1) + 2 * c + (b >> 1)
            parts.append(in_ref[source, 0:8, :].astype(f32))
        for g in range(3):
            line = None
            for b in range(4):
                part = pltpu.roll(parts[b], (32 * (b - g)) % 128, 1) if b != g else parts[b]
                line = part if line is None else jnp.where(band == b, part, line)
            rows[g].append(line)
    lines = jnp.concatenate([jnp.concatenate(r, axis=1) for r in rows], axis=0)
    scale = lax.rsqrt(jnp.sum(lines * lines, axis=1, keepdims=True) * (1.0 / D) + EPS)
    level2_ref[...] = (lines * scale).astype(bf16)

    tails = in_ref[:, 8:16, :].astype(f32)
    squares = jnp.sum(tails, axis=0)
    squares = jnp.concatenate([squares[c : c + 1] for c in range(6)], axis=1)
    scale = lax.rsqrt(squares * (1.0 / D) + EPS)
    named = 8.0 * tails[:, 6:7] + tails[:, 7:8]
    named = jnp.concatenate(
        [pltpu.roll(named[n], (ROWS * n) % 128, 1) if n % N_MP else named[n] for n in range(2 * N_MP)], axis=0
    )
    parent = []
    for c in range(6):
        place = iota((2 * N_MP, 128), 1) + 128 * c
        mine = ((place >> 3) * 171) >> 9 == iota((2 * N_MP, 128), 0)
        parent.append(jnp.sum(jnp.where(mine, named, 0.0), axis=0, keepdims=True))
    parent = jnp.concatenate(parent, axis=1).astype(i32)
    device = ((parent >> 3) & 15) * N_MP + (parent >> 7)
    key = rows_of((device * 2 + (parent & 1)).astype(f32), N_DP * N_MP)

    weighted = (keep_ref[0:32, :] * scale).astype(bf16).astype(f32) * keep_ref[32:33, :]
    part = (parent >> 1) & 3
    both = jnp.concatenate([jnp.where(part == s, weighted, 0.0) for s in range(4)], axis=0)
    high = both.astype(bf16)
    low = (both - high.astype(f32)).astype(bf16)
    total = dot_nt(key, jnp.concatenate([high, low], axis=0))
    out_ref[...] = (total[:, :128] + total[:, 128:]).astype(bf16)


def spread_kernel(in_ref, out_ref):
    total = jnp.sum(in_ref[...].astype(f32).reshape(N_MP, 32, 128), axis=0).reshape(4, 8, 128)
    band, part = iota((4, 8, 128), 2) >> 5, iota((4, 8, 128), 1) >> 1
    turned = [total] + [pltpu.roll(total, 32 * d, 2) for d in range(1, 4)]
    out = jnp.zeros((4, 8, 128), f32)
    for b, j in enumerate((0, 2, 1, 3)):
        for s in range(4):
            piece = turned[(b - s) % 4]
            if s != j:
                piece = pltpu.roll(piece, (2 * (s - j)) % 8, 1)
            out = jnp.where((band == b) & (part == s), piece, out)
    out = jnp.where(lax.axis_index("core") == 1, pltpu.roll(out, 32, 2), out)
    out_ref[...] = jnp.broadcast_to(out.reshape(32, 128).astype(bf16)[None], (N_DP, 32, 128))


def finish_kernel(in_ref, out_ref):
    band = iota((N_MP, 8, 128), 2) >> 5
    tiles = []
    square = jnp.zeros((N_MP, 8, 128), f32)
    for t in range(4):
        block = pl.ds(8 * t, 8)
        first = jnp.concatenate([in_ref[2 * p : 2 * p + 1, block, :] for p in range(N_MP)], axis=0).astype(f32)
        second = jnp.concatenate([in_ref[2 * p + 1 : 2 * p + 2, block, :] for p in range(N_MP)], axis=0).astype(f32)
        even = (band & 1) == 0
        tiles.append(jnp.where(even, first, second))
        tiles.append(pltpu.roll(jnp.where(even, second, first), 96, 2))
        square = square + tiles[-1] * tiles[-1] + tiles[-2] * tiles[-2]
    scale = lax.rsqrt(jnp.sum(square, axis=2, keepdims=True) * (1.0 / D) + EPS)
    for c in range(8):
        out_ref[:, 128 * c : 128 * (c + 1)] = (tiles[c] * scale).reshape(K3_MP, 128).astype(bf16)


def call(kernel, out, *args, far=(), scratch=()):
    vmem = pl.BlockSpec(memory_space=pltpu.VMEM)
    many = isinstance(out, tuple)
    return pl.pallas_call(
        kernel,
        out_shape=out,
        in_specs=[pl.BlockSpec(memory_space=pltpu.HBM)] * len(far) + [vmem] * len(args),
        out_specs=(vmem,) * len(out) if many else vmem,
        scratch_shapes=scratch,
        compiler_params=pltpu.CompilerParams(vmem_limit_bytes=48 * 1024 * 1024),
    )(*(pltpu.with_memory_space_constraint(x, pltpu.HBM) for x in far), *args)


def shape(dims, dtype):
    return jax.ShapeDtypeStruct(dims, dtype)


def exchange(x, axis):
    return lax.all_to_all(x, axis, 0, 0, tiled=True)


def body(points, point_cluster, cluster_parent):
    rows = N_DP * STRIDE
    sent = call(
        sort_kernel,
        shape((rows, 128), bf16),
        far=(point_cluster.T, points.T),
        scratch=(
            pltpu.VMEM((1, PTS), i32),
            pltpu.VMEM((FEAT, PTS), bf16),
            pltpu.VMEM((rows, 128), f32),
            pltpu.SemaphoreType.DMA((2,)),
        ),
    )
    got = exchange(sent.reshape(N_DP, STRIDE // 2, 2, 128), ("pair", "core")).reshape(rows, 128)
    sums, keep = call(
        sum_kernel,
        (shape((2 * N_MP, 16, 128), bf16), shape((40, 2 * GROUP), f32)),
        got,
        far=(cluster_parent.T,),
        scratch=(
            pltpu.VMEM((1, ROWS), i32),
            pltpu.VMEM((rows, 128), f32),
            pltpu.SemaphoreType.DMA(()),
        ),
    )
    peers = N_DP // 2 * N_MP
    level2, partial = call(
        unit_kernel,
        (shape((ROWS, D), bf16), shape((2 * peers, 128), bf16)),
        exchange(sums, ("core", "mp")),
        keep,
    )
    parts = exchange(partial.reshape(peers, 2, 128), ("pair", "mp")).reshape(2 * peers, 128)
    parents = call(spread_kernel, shape((N_DP, 32, 128), bf16), parts)
    level3 = call(finish_kernel, shape((K3_MP, D), bf16), exchange(parents, ("pair", "core")))
    return (level2, level3)


def solution(mesh):
    pairs = Mesh(mesh.devices.reshape(N_DP // 2, 2, N_MP), ("pair", "core", "mp"))
    dp = ("pair", "core")
    placed = (P(dp, "mp"), P(dp, None), P((*dp, "mp"), None))
    return jax.shard_map(
        body,
        mesh=pairs,
        in_specs=placed,
        out_specs=(P((*dp, "mp"), None), P("mp", None)),
        check_vma=False,
    )
```

```python
import jax
import jax.numpy as jnp
from jax import lax
from jax.experimental import pallas as pl
from jax.experimental.pallas import tpu as pltpu
from jax.sharding import Mesh
from jax.sharding import PartitionSpec as P

N_DP = 32
N_MP = 16
PTS = 2048
FEAT = 64
ROWS = 24
GROUP = ROWS * N_MP
D = 1024
K3 = 2048
K3_MP = 128
EPS = 1e-06
STRIDE = 34

f32 = jnp.float32
bf16 = jnp.bfloat16
i32 = jnp.int32


def iota(shape, dim):
    return lax.broadcasted_iota(i32, shape, dim)


def rows_of(row, n):
    one, zero = jnp.ones((), bf16), jnp.zeros((), bf16)
    blocks = []
    for at in range(0, n, 256):
        number = iota((min(256, n - at), row.shape[1]), 0).astype(f32).astype(bf16)
        blocks.append(jnp.where(number == (row - at).astype(bf16), one, zero))
    return jnp.concatenate(blocks, axis=0)


def hot(mask):
    return jnp.where(mask, 1.0, 0.0).astype(bf16)


def dot_nt(a, b):
    return lax.dot_general(a, b, (((1,), (1,)), ((), ())), preferred_element_type=f32)


def dot_nn(a, b):
    return lax.dot_general(a, b, (((1,), (0,)), ((), ())), preferred_element_type=f32)


def sort_kernel(labels_hbm, points_hbm, out_ref, labels_ref, points_ref, rows_ref, sems):
    fetch_labels = pltpu.make_async_copy(labels_hbm, labels_ref, sems.at[0])
    fetch_points = pltpu.make_async_copy(points_hbm, points_ref, sems.at[1])
    fetch_labels.start()
    fetch_points.start()
    fetch_labels.wait()
    labels = labels_ref[...]
    group = ((labels >> 7) * 171) >> 9
    local = labels - group * GROUP
    member = jnp.where(iota((N_DP, PTS), 0) == group, 1.0, 0.0)
    member16 = member.astype(bf16)
    width = 256
    n_chunks = PTS // width
    stacked = jnp.concatenate(
        [member16[:, c * width : (c + 1) * width] for c in range(n_chunks)], axis=0
    )
    before = hot(iota((width, 2 * width), 0) < iota((width, 2 * width), 1))
    prefix = dot_nn(stacked, before)
    base = jnp.zeros((N_DP, width), f32)
    ranks = []
    for c in range(n_chunks):
        part = prefix[c * N_DP : (c + 1) * N_DP]
        inside = member[:, c * width : (c + 1) * width]
        ranks.append(jnp.sum(inside * (part[:, :width] + base), axis=0, keepdims=True))
        base = base + part[:, width:]
    rank = jnp.concatenate(ranks, axis=1).astype(i32)
    r1 = rank & 7
    r2 = rank >> 3
    key = rows_of((group * 8 + r2).astype(f32), N_DP * 8)

    line = iota((N_DP, PTS), 0)
    digit = jnp.where((line & 1) == 0, local >> 3, local & 7).astype(f32)
    digit = jnp.where((line >> 1) == (group >> 1), digit, 0.0).astype(bf16)
    place = lax.axis_index("pair") * 2 + lax.axis_index("core")
    slot = (group & 1) * 4 + (r1 & 3)
    spot = (16 * (place + slot) + (r1 >> 2) * 8 + r2) & 127

    fetch_points.wait()
    points = points_ref[...]
    masks = [hot(r1 == r) for r in range(8)]
    split = jnp.concatenate(
        [points[32 * half : 32 * half + 32] * masks[r] for half in range(2) for r in range(8)], axis=0
    )
    moved = dot_nt(key, split)
    tags = dot_nt(digit, rows_of(spot.astype(f32), 128))
    for d in range(N_DP):
        pair, half = d >> 1, d & 1
        for own in range(2):
            for h in range(2):
                at = STRIDE * d + 16 * own + 8 * h
                line, lane = 8 * (2 * pair + own), 256 * half + 128 * h
                rows_ref[at : at + 8, :] = moved[line : line + 8, lane : lane + 128]
        rows_ref[STRIDE * d + 32 : STRIDE * d + 34, :] = tags[2 * pair : 2 * pair + 2]
    out_ref[...] = rows_ref[...].astype(bf16)


def sum_kernel(parent_hbm, in_ref, out_ref, keep_ref, parent_ref, rows_ref, sem):
    fetch = pltpu.make_async_copy(parent_hbm, parent_ref, sem)
    fetch.start()
    rows_ref[...] = in_ref[...].astype(f32)
    tags = 8.0 * rows_ref[pl.ds(32, N_DP, stride=STRIDE), :] + rows_ref[pl.ds(33, N_DP, stride=STRIDE), :]
    mine = iota((8, 128), 1) >> 4 == iota((8, 128), 0)
    quarter = iota((GROUP, 128), 1) >> 5
    half = N_DP * 16
    sides = [hot(iota((1, 128), 1) >> 5 == s) for s in range(4)]
    wides, squares = [], []
    for own in range(2):
        data = jnp.concatenate(
            [rows_ref[STRIDE * i + 16 * own : STRIDE * i + 16 * own + 16, :] for i in range(N_DP)], axis=0
        ).astype(bf16)
        labels = []
        for s in range(4):
            slot = own * 4 + s
            turned = pltpu.roll(tags, 128 - 16 * slot, 1) if slot else tags
            labels += [
                jnp.sum(jnp.where(mine, turned[8 * t : 8 * t + 8], 0.0), axis=0, keepdims=True)
                for t in range(4)
            ]
        split = jnp.concatenate([data * side for side in sides], axis=0)
        split = jnp.concatenate([split, jnp.ones((4 * half, 128), bf16)], axis=1)
        result = dot_nn(rows_of(jnp.concatenate(labels, axis=1), GROUP), split)
        sums, counts = result[:, :128], result[:, 128:]
        sums = sums + pltpu.roll(sums, 64, 1)
        sums = sums + pltpu.roll(sums, 32, 1)
        turned = jnp.where(quarter == 0, sums, counts).T
        keep_ref[:, own * GROUP : (own + 1) * GROUP] = turned[:40]
        square = jnp.sum(turned[:32] * turned[:32], axis=0, keepdims=True)
        squares += [square[:, 128 * c : 128 * (c + 1)] for c in range(3)]
        sums = sums.reshape(N_MP, 3, 8, 128)
        band = iota((N_MP, 8, 128), 2) >> 5
        wide = jnp.where(band == 0, sums[:, 0], jnp.where(band == 1, sums[:, 1], sums[:, 2]))
        wides.append(wide.astype(bf16))
    fetch.wait()
    parent = parent_ref[...]
    parent = jnp.concatenate([parent >> 3, parent & 7], axis=0).astype(f32)
    parent = jnp.concatenate([parent, jnp.zeros((2, 128 - ROWS), f32)], axis=1)
    tail = jnp.concatenate(squares + [parent], axis=0).astype(bf16)
    for own in range(2):
        block = slice(N_MP * own, N_MP * (own + 1))
        out_ref[block, 0:8, :] = wides[own]
    out_ref[:, 8:16, :] = jnp.broadcast_to(tail[None], (2 * N_MP, 8, 128))


def unit_kernel(in_ref, keep_ref, level2_ref, out_ref):
    band = iota((8, 128), 1) >> 5
    rows = ([], [], [])
    for c in range(N_MP // 2):
        parts = []
        for b in range(4):
            source = N_MP * (b & 1) + 2 * c + (b >> 1)
            parts.append(in_ref[source, 0:8, :].astype(f32))
        for g in range(3):
            line = None
            for b in range(4):
                part = pltpu.roll(parts[b], (32 * (b - g)) % 128, 1) if b != g else parts[b]
                line = part if line is None else jnp.where(band == b, part, line)
            rows[g].append(line)
    lines = jnp.concatenate([jnp.concatenate(r, axis=1) for r in rows], axis=0)
    scale = lax.rsqrt(jnp.sum(lines * lines, axis=1, keepdims=True) * (1.0 / D) + EPS)
    level2_ref[...] = (lines * scale).astype(bf16)

    tails = in_ref[:, 8:16, :].astype(f32)
    squares = jnp.sum(tails, axis=0)
    squares = jnp.concatenate([squares[c : c + 1] for c in range(6)], axis=1)
    scale = lax.rsqrt(squares * (1.0 / D) + EPS)
    named = 8.0 * tails[:, 6:7] + tails[:, 7:8]
    named = jnp.concatenate(
        [pltpu.roll(named[n], (ROWS * n) % 128, 1) if n % N_MP else named[n] for n in range(2 * N_MP)], axis=0
    )
    parent = []
    for c in range(6):
        place = iota((2 * N_MP, 128), 1) + 128 * c
        mine = ((place >> 3) * 171) >> 9 == iota((2 * N_MP, 128), 0)
        parent.append(jnp.sum(jnp.where(mine, named, 0.0), axis=0, keepdims=True))
    parent = jnp.concatenate(parent, axis=1).astype(i32)
    device = ((parent >> 3) & 15) * N_MP + (parent >> 7)
    key = rows_of((device * 2 + (parent & 1)).astype(f32), N_DP * N_MP)

    weighted = (keep_ref[0:32, :] * scale).astype(bf16).astype(f32) * keep_ref[32:33, :]
    part = (parent >> 1) & 3
    both = jnp.concatenate([jnp.where(part == s, weighted, 0.0) for s in range(4)], axis=0)
    high = both.astype(bf16)
    low = (both - high.astype(f32)).astype(bf16)
    total = dot_nt(key, jnp.concatenate([high, low], axis=0))
    out_ref[...] = (total[:, :128] + total[:, 128:]).astype(bf16)


def spread_kernel(in_ref, out_ref):
    total = jnp.sum(in_ref[...].astype(f32).reshape(N_MP, 32, 128), axis=0).reshape(4, 8, 128)
    band, part = iota((4, 8, 128), 2) >> 5, iota((4, 8, 128), 1) >> 1
    turned = [total] + [pltpu.roll(total, 32 * d, 2) for d in range(1, 4)]
    out = jnp.zeros((4, 8, 128), f32)
    for b, j in enumerate((0, 2, 1, 3)):
        for s in range(4):
            piece = turned[(b - s) % 4]
            if s != j:
                piece = pltpu.roll(piece, (2 * (s - j)) % 8, 1)
            out = jnp.where((band == b) & (part == s), piece, out)
    out = jnp.where(lax.axis_index("core") == 1, pltpu.roll(out, 32, 2), out)
    out_ref[...] = jnp.broadcast_to(out.reshape(32, 128).astype(bf16)[None], (N_DP, 32, 128))


def finish_kernel(in_ref, level2_ref, out_hbm, level2_hbm, out_ref, sems):
    stores = [pltpu.make_async_copy(level2_ref, level2_hbm, sems.at[2])]
    stores[0].start()
    band = iota((N_MP, 8, 128), 2) >> 5
    tiles = []
    square = jnp.zeros((N_MP, 8, 128), f32)
    for t in range(4):
        block = pl.ds(8 * t, 8)
        first = jnp.concatenate([in_ref[2 * p : 2 * p + 1, block, :] for p in range(N_MP)], axis=0).astype(f32)
        second = jnp.concatenate([in_ref[2 * p + 1 : 2 * p + 2, block, :] for p in range(N_MP)], axis=0).astype(f32)
        even = (band & 1) == 0
        tiles.append(jnp.where(even, first, second))
        tiles.append(pltpu.roll(jnp.where(even, second, first), 96, 2))
        square = square + tiles[-1] * tiles[-1] + tiles[-2] * tiles[-2]
    scale = lax.rsqrt(jnp.sum(square, axis=2, keepdims=True) * (1.0 / D) + EPS)
    for n in range(2):
        block = pl.ds(64 * n, 64)
        for c in range(8):
            part = tiles[c][8 * n : 8 * n + 8] * scale[8 * n : 8 * n + 8]
            out_ref[block, 128 * c : 128 * (c + 1)] = part.reshape(64, 128).astype(bf16)
        stores.append(pltpu.make_async_copy(out_ref.at[block], out_hbm.at[block], sems.at[n]))
        stores[-1].start()
    for store in stores:
        store.wait()


def call(kernel, out, *args, far=(), scratch=(), spaces=(pltpu.VMEM,)):
    many = isinstance(out, tuple)
    results = tuple(pl.BlockSpec(memory_space=space) for space in spaces)
    return pl.pallas_call(
        kernel,
        out_shape=out,
        in_specs=[pl.BlockSpec(memory_space=pltpu.HBM)] * len(far)
        + [pl.BlockSpec(memory_space=pltpu.VMEM)] * len(args),
        out_specs=results if many else results[0],
        scratch_shapes=scratch,
        compiler_params=pltpu.CompilerParams(vmem_limit_bytes=48 * 1024 * 1024),
    )(*(pltpu.with_memory_space_constraint(x, pltpu.HBM) for x in far), *args)


def shape(dims, dtype):
    return jax.ShapeDtypeStruct(dims, dtype)


def exchange(x, axis):
    return lax.all_to_all(x, axis, 0, 0, tiled=True)


def body(points, point_cluster, cluster_parent):
    rows = N_DP * STRIDE
    sent = call(
        sort_kernel,
        shape((rows, 128), bf16),
        far=(point_cluster.T, points.T),
        scratch=(
            pltpu.VMEM((1, PTS), i32),
            pltpu.VMEM((FEAT, PTS), bf16),
            pltpu.VMEM((rows, 128), f32),
            pltpu.SemaphoreType.DMA((2,)),
        ),
    )
    got = exchange(sent.reshape(N_DP, STRIDE // 2, 2, 128), ("pair", "core")).reshape(rows, 128)
    sums, keep = call(
        sum_kernel,
        (shape((2 * N_MP, 16, 128), bf16), shape((40, 2 * GROUP), f32)),
        got,
        far=(cluster_parent.T,),
        scratch=(
            pltpu.VMEM((1, ROWS), i32),
            pltpu.VMEM((rows, 128), f32),
            pltpu.SemaphoreType.DMA(()),
        ),
        spaces=(pltpu.VMEM, pltpu.VMEM),
    )
    peers = N_DP // 2 * N_MP
    level2, partial = call(
        unit_kernel,
        (shape((ROWS, D), bf16), shape((2 * peers, 128), bf16)),
        exchange(sums, ("core", "mp")),
        keep,
        spaces=(pltpu.VMEM, pltpu.VMEM),
    )
    parts = exchange(partial.reshape(peers, 2, 128), ("pair", "mp")).reshape(2 * peers, 128)
    parents = call(spread_kernel, shape((N_DP, 32, 128), bf16), parts)
    level3, level2 = call(
        finish_kernel,
        (shape((K3_MP, D), bf16), shape((ROWS, D), bf16)),
        exchange(parents, ("pair", "core")),
        level2,
        scratch=(pltpu.VMEM((K3_MP, D), bf16), pltpu.SemaphoreType.DMA((3,))),
        spaces=(pltpu.HBM, pltpu.HBM),
    )
    return (level2, level3)


def solution(mesh):
    pairs = Mesh(mesh.devices.reshape(N_DP // 2, 2, N_MP), ("pair", "core", "mp"))
    dp = ("pair", "core")
    placed = (P(dp, "mp"), P(dp, None), P((*dp, "mp"), None))
    return jax.shard_map(
        body,
        mesh=pairs,
        in_specs=placed,
        out_specs=(P((*dp, "mp"), None), P("mp", None)),
        check_vma=False,
    )
```

```python
import jax
import jax.numpy as jnp
from jax import lax
from jax.experimental import pallas as pl
from jax.experimental.pallas import tpu as pltpu
from jax.sharding import Mesh
from jax.sharding import PartitionSpec as P

N_DP = 32
N_MP = 16
PTS = 2048
FEAT = 64
ROWS = 24
GROUP = ROWS * N_MP
D = 1024
K3 = 2048
K3_MP = 128
EPS = 1e-06
STRIDE = 34

f32 = jnp.float32
bf16 = jnp.bfloat16
i32 = jnp.int32


def iota(shape, dim):
    return lax.broadcasted_iota(i32, shape, dim)


def rows_of(row, n):
    one, zero = jnp.ones((), bf16), jnp.zeros((), bf16)
    blocks = []
    for at in range(0, n, 256):
        number = iota((min(256, n - at), row.shape[1]), 0).astype(f32).astype(bf16)
        blocks.append(jnp.where(number == (row - at).astype(bf16), one, zero))
    return jnp.concatenate(blocks, axis=0)


def hot(mask):
    return jnp.where(mask, 1.0, 0.0).astype(bf16)


def dot_nt(a, b):
    return lax.dot_general(a, b, (((1,), (1,)), ((), ())), preferred_element_type=f32)


def dot_nn(a, b):
    return lax.dot_general(a, b, (((1,), (0,)), ((), ())), preferred_element_type=f32)


def sort_kernel(labels_hbm, points_hbm, out_ref, labels_ref, points_ref, rows_ref, sems):
    fetch_labels = pltpu.make_async_copy(labels_hbm, labels_ref, sems.at[0])
    fetch_points = pltpu.make_async_copy(points_hbm, points_ref, sems.at[1])
    fetch_labels.start()
    fetch_points.start()
    fetch_labels.wait()
    labels = labels_ref[...]
    group = ((labels >> 7) * 171) >> 9
    local = labels - group * GROUP
    member = jnp.where(iota((N_DP, PTS), 0) == group, 1.0, 0.0)
    member16 = member.astype(bf16)
    width = 256
    n_chunks = PTS // width
    stacked = jnp.concatenate(
        [member16[:, c * width : (c + 1) * width] for c in range(n_chunks)], axis=0
    )
    before = hot(iota((width, 2 * width), 0) < iota((width, 2 * width), 1))
    prefix = dot_nn(stacked, before)
    base = jnp.zeros((N_DP, width), f32)
    ranks = []
    for c in range(n_chunks):
        part = prefix[c * N_DP : (c + 1) * N_DP]
        inside = member[:, c * width : (c + 1) * width]
        ranks.append(jnp.sum(inside * (part[:, :width] + base), axis=0, keepdims=True))
        base = base + part[:, width:]
    rank = jnp.concatenate(ranks, axis=1).astype(i32)
    r1 = rank & 7
    r2 = rank >> 3
    key = rows_of((group * 8 + r2).astype(f32), N_DP * 8)

    line = iota((N_DP, PTS), 0)
    digit = jnp.where((line & 1) == 0, local >> 3, local & 7).astype(f32)
    digit = jnp.where((line >> 1) == (group >> 1), digit, 0.0).astype(bf16)
    place = lax.axis_index("pair") * 2 + lax.axis_index("core")
    slot = (group & 1) * 4 + (r1 & 3)
    spot = (16 * (place + slot) + (r1 >> 2) * 8 + r2) & 127

    fetch_points.wait()
    points = points_ref[...]
    masks = [hot(r1 == r) for r in range(8)]
    split = jnp.concatenate(
        [points[32 * half : 32 * half + 32] * masks[r] for half in range(2) for r in range(8)], axis=0
    )
    moved = dot_nt(key, split)
    tags = dot_nt(digit, rows_of(spot.astype(f32), 128))
    for d in range(N_DP):
        pair, half = d >> 1, d & 1
        for own in range(2):
            for h in range(2):
                at = STRIDE * d + 16 * own + 8 * h
                line, lane = 8 * (2 * pair + own), 256 * half + 128 * h
                rows_ref[at : at + 8, :] = moved[line : line + 8, lane : lane + 128]
        rows_ref[STRIDE * d + 32 : STRIDE * d + 34, :] = tags[2 * pair : 2 * pair + 2]
    out_ref[...] = rows_ref[...].astype(bf16)


def sum_kernel(parent_hbm, in_ref, out_ref, keep_ref, count_ref, parent_ref, rows_ref, sem):
    fetch = pltpu.make_async_copy(parent_hbm, parent_ref, sem)
    fetch.start()
    rows_ref[...] = in_ref[...].astype(f32)
    tags = 8.0 * rows_ref[pl.ds(32, N_DP, stride=STRIDE), :] + rows_ref[pl.ds(33, N_DP, stride=STRIDE), :]
    mine = iota((8, 128), 1) >> 4 == iota((8, 128), 0)
    quarter = iota((GROUP, 128), 1) >> 5
    half = N_DP * 16
    sides = [hot(iota((1, 128), 1) >> 5 == s) for s in range(4)]
    wides, squares = [], []
    for own in range(2):
        data = jnp.concatenate(
            [rows_ref[STRIDE * i + 16 * own : STRIDE * i + 16 * own + 16, :] for i in range(N_DP)], axis=0
        ).astype(bf16)
        labels = []
        for s in range(4):
            slot = own * 4 + s
            turned = pltpu.roll(tags, 128 - 16 * slot, 1) if slot else tags
            labels += [
                jnp.sum(jnp.where(mine, turned[8 * t : 8 * t + 8], 0.0), axis=0, keepdims=True)
                for t in range(4)
            ]
        split = jnp.concatenate([data * side for side in sides], axis=0)
        split = jnp.concatenate([split, jnp.ones((4 * half, 128), bf16)], axis=1)
        result = dot_nn(rows_of(jnp.concatenate(labels, axis=1), GROUP), split)
        sums, counts = result[:, :128], result[:, 128:]
        sums = sums + pltpu.roll(sums, 64, 1)
        sums = sums + pltpu.roll(sums, 32, 1)
        turned = jnp.where(quarter == 0, sums, counts).T
        keep_ref[:, own * GROUP : (own + 1) * GROUP] = turned[:32]
        count_ref[:, own * GROUP : (own + 1) * GROUP] = turned[32:40]
        square = jnp.sum(turned[:32] * turned[:32], axis=0, keepdims=True)
        squares += [square[:, 128 * c : 128 * (c + 1)] for c in range(3)]
        sums = sums.reshape(N_MP, 3, 8, 128)
        band = iota((N_MP, 8, 128), 2) >> 5
        wide = jnp.where(band == 0, sums[:, 0], jnp.where(band == 1, sums[:, 1], sums[:, 2]))
        wides.append(wide.astype(bf16))
    fetch.wait()
    parent = parent_ref[...]
    parent = jnp.concatenate([parent >> 3, parent & 7], axis=0).astype(f32)
    parent = jnp.concatenate([parent, jnp.zeros((2, 128 - ROWS), f32)], axis=1)
    tail = jnp.concatenate(squares + [parent], axis=0).astype(bf16)
    for own in range(2):
        block = slice(N_MP * own, N_MP * (own + 1))
        out_ref[block, 0:8, :] = wides[own]
    out_ref[:, 8:16, :] = jnp.broadcast_to(tail[None], (2 * N_MP, 8, 128))


def unit_kernel(in_ref, keep_ref, other_ref, count_ref, level2_ref, out_ref):
    band = iota((8, 128), 1) >> 5
    rows = ([], [], [])
    for c in range(N_MP // 2):
        parts = []
        for b in range(4):
            source = N_MP * (b & 1) + 2 * c + (b >> 1)
            parts.append(in_ref[source, 0:8, :].astype(f32))
        for g in range(3):
            line = None
            for b in range(4):
                part = pltpu.roll(parts[b], (32 * (b - g)) % 128, 1) if b != g else parts[b]
                line = part if line is None else jnp.where(band == b, part, line)
            rows[g].append(line)
    lines = jnp.concatenate([jnp.concatenate(r, axis=1) for r in rows], axis=0)
    scale = lax.rsqrt(jnp.sum(lines * lines, axis=1, keepdims=True) * (1.0 / D) + EPS)
    level2_ref[...] = (lines * scale).astype(bf16)

    tails = in_ref[:, 8:16, :].astype(f32)
    squares = jnp.sum(tails, axis=0)
    squares = jnp.concatenate([squares[c : c + 1] for c in range(6)], axis=1)
    scale = lax.rsqrt(squares * (1.0 / D) + EPS)
    named = 8.0 * tails[:, 6:7] + tails[:, 7:8]
    named = jnp.concatenate(
        [pltpu.roll(named[n], (ROWS * n) % 128, 1) if n % N_MP else named[n] for n in range(2 * N_MP)], axis=0
    )
    parent = []
    for c in range(6):
        place = iota((2 * N_MP, 128), 1) + 128 * c
        mine = ((place >> 3) * 171) >> 9 == iota((2 * N_MP, 128), 0)
        parent.append(jnp.sum(jnp.where(mine, named, 0.0), axis=0, keepdims=True))
    parent = jnp.concatenate(parent, axis=1).astype(i32)
    side = lax.axis_index("xl")
    line = (((parent >> 3) & 15) * 8 + (parent >> 8)) * 4 + (parent & 3)
    line = jnp.where(((parent >> 7) & 1) == side, line, -1)
    key = rows_of(line.astype(f32), N_DP * N_MP)

    factor = count_ref[0:1, :]
    own = (keep_ref[...] * scale).astype(bf16).astype(f32) * factor
    other = (other_ref[...] * scale).astype(bf16).astype(f32) * factor
    part = (parent >> 2) & 1
    both = jnp.concatenate(
        [
            jnp.where(part == s, block, 0.0)
            for block in (jnp.where(side == 0, own, other), jnp.where(side == 0, other, own))
            for s in range(2)
        ],
        axis=0,
    )
    high = both.astype(bf16)
    low = (both - high.astype(f32)).astype(bf16)
    total = dot_nt(key, jnp.concatenate([high, low], axis=0))
    out_ref[...] = (total[:, :128] + total[:, 128:]).astype(bf16)


def spread_kernel(in_ref, out_ref):
    total = jnp.sum(in_ref[...].astype(f32).reshape(N_DP // 2, 32, 128), axis=0).reshape(4, 8, 128)
    odd, lower = (iota((4, 8, 128), 2) >> 5) & 1, iota((4, 8, 128), 1) >> 2
    swapped = pltpu.roll(total, 4, 1)
    swapped = jnp.where(lower == 0, pltpu.roll(swapped, 32, 2), pltpu.roll(swapped, 96, 2))
    out = jnp.where(odd == lower, total, swapped)
    out = jnp.where(lax.axis_index("core") == 1, pltpu.roll(out, 32, 2), out)
    out_ref[...] = jnp.broadcast_to(out.reshape(32, 128).astype(bf16)[None], (N_DP, 32, 128))


def finish_kernel(in_ref, level2_ref, out_hbm, level2_hbm, out_ref, sems):
    stores = [pltpu.make_async_copy(level2_ref, level2_hbm, sems.at[2])]
    stores[0].start()
    band = iota((N_MP, 8, 128), 2) >> 5
    tiles = []
    square = jnp.zeros((N_MP, 8, 128), f32)
    for t in range(4):
        block = pl.ds(8 * t, 8)
        first = jnp.concatenate([in_ref[2 * p : 2 * p + 1, block, :] for p in range(N_MP)], axis=0).astype(f32)
        second = jnp.concatenate([in_ref[2 * p + 1 : 2 * p + 2, block, :] for p in range(N_MP)], axis=0).astype(f32)
        even = (band & 1) == 0
        tiles.append(jnp.where(even, first, second))
        tiles.append(pltpu.roll(jnp.where(even, second, first), 96, 2))
        square = square + tiles[-1] * tiles[-1] + tiles[-2] * tiles[-2]
    scale = lax.rsqrt(jnp.sum(square, axis=2, keepdims=True) * (1.0 / D) + EPS)
    for n in range(2):
        block = pl.ds(64 * n, 64)
        for c in range(8):
            part = tiles[c][8 * n : 8 * n + 8] * scale[8 * n : 8 * n + 8]
            out_ref[block, 128 * c : 128 * (c + 1)] = part.reshape(64, 128).astype(bf16)
        stores.append(pltpu.make_async_copy(out_ref.at[block], out_hbm.at[block], sems.at[n]))
        stores[-1].start()
    for store in stores:
        store.wait()


def call(kernel, out, *args, far=(), scratch=(), spaces=(pltpu.VMEM,)):
    many = isinstance(out, tuple)
    results = tuple(pl.BlockSpec(memory_space=space) for space in spaces)
    return pl.pallas_call(
        kernel,
        out_shape=out,
        in_specs=[pl.BlockSpec(memory_space=pltpu.HBM)] * len(far)
        + [pl.BlockSpec(memory_space=pltpu.VMEM)] * len(args),
        out_specs=results if many else results[0],
        scratch_shapes=scratch,
        compiler_params=pltpu.CompilerParams(vmem_limit_bytes=48 * 1024 * 1024),
    )(*(pltpu.with_memory_space_constraint(x, pltpu.HBM) for x in far), *args)


def shape(dims, dtype):
    return jax.ShapeDtypeStruct(dims, dtype)


def exchange(x, axis):
    return lax.all_to_all(x, axis, 0, 0, tiled=True)


def body(points, point_cluster, cluster_parent):
    rows = N_DP * STRIDE
    sent = call(
        sort_kernel,
        shape((rows, 128), bf16),
        far=(point_cluster.T, points.T),
        scratch=(
            pltpu.VMEM((1, PTS), i32),
            pltpu.VMEM((FEAT, PTS), bf16),
            pltpu.VMEM((rows, 128), f32),
            pltpu.SemaphoreType.DMA((2,)),
        ),
    )
    got = exchange(sent.reshape(N_DP, STRIDE // 2, 2, 128), ("pair", "core")).reshape(rows, 128)
    sums, keep, counts = call(
        sum_kernel,
        (shape((2 * N_MP, 16, 128), bf16), shape((32, 2 * GROUP), f32), shape((8, 2 * GROUP), f32)),
        got,
        far=(cluster_parent.T,),
        scratch=(
            pltpu.VMEM((1, ROWS), i32),
            pltpu.VMEM((rows, 128), f32),
            pltpu.SemaphoreType.DMA(()),
        ),
        spaces=(pltpu.VMEM,) * 3,
    )
    other = lax.ppermute(keep, "xl", [(0, 1), (1, 0)])
    peers = N_DP // 2 * N_MP // 2
    level2, partial = call(
        unit_kernel,
        (shape((ROWS, D), bf16), shape((4 * peers, 128), bf16)),
        exchange(sums, ("core", "y", "xl")),
        keep,
        other,
        counts,
        spaces=(pltpu.VMEM, pltpu.VMEM),
    )
    parts = exchange(partial.reshape(peers, 4, 128), ("pair", "y")).reshape(4 * peers, 128)
    parents = call(spread_kernel, shape((N_DP, 32, 128), bf16), parts)
    level3, level2 = call(
        finish_kernel,
        (shape((K3_MP, D), bf16), shape((ROWS, D), bf16)),
        exchange(parents, ("pair", "core")),
        level2,
        scratch=(pltpu.VMEM((K3_MP, D), bf16), pltpu.SemaphoreType.DMA((3,))),
        spaces=(pltpu.HBM, pltpu.HBM),
    )
    return (level2, level3)


def solution(mesh):
    split = Mesh(mesh.devices.reshape(N_DP // 2, 2, N_MP // 2, 2), ("pair", "core", "y", "xl"))
    dp, mp = ("pair", "core"), ("y", "xl")
    placed = (P(dp, mp), P(dp, None), P((*dp, *mp), None))
    return jax.shard_map(
        body,
        mesh=split,
        in_specs=placed,
        out_specs=(P((*dp, *mp), None), P(mp, None)),
        check_vma=False,
    )
```

```python
import jax
import jax.numpy as jnp
from jax import lax
from jax.experimental import pallas as pl
from jax.experimental.pallas import tpu as pltpu
from jax.sharding import Mesh
from jax.sharding import PartitionSpec as P

N_DP = 32
N_MP = 16
PTS = 2048
FEAT = 64
ROWS = 24
GROUP = ROWS * N_MP
D = 1024
K3 = 2048
K3_MP = 128
EPS = 1e-06
STRIDE = 34

f32 = jnp.float32
bf16 = jnp.bfloat16
i32 = jnp.int32


def iota(shape, dim):
    return lax.broadcasted_iota(i32, shape, dim)


def rows_of(row, n):
    one, zero = jnp.ones((), bf16), jnp.zeros((), bf16)
    blocks = []
    for at in range(0, n, 256):
        number = iota((min(256, n - at), row.shape[1]), 0).astype(f32).astype(bf16)
        blocks.append(jnp.where(number == (row - at).astype(bf16), one, zero))
    return jnp.concatenate(blocks, axis=0)


def hot(mask):
    return jnp.where(mask, 1.0, 0.0).astype(bf16)


def dot_nt(a, b):
    return lax.dot_general(a, b, (((1,), (1,)), ((), ())), preferred_element_type=f32)


def dot_nn(a, b):
    return lax.dot_general(a, b, (((1,), (0,)), ((), ())), preferred_element_type=f32)


def sort_kernel(labels_hbm, points_hbm, out_ref, labels_ref, points_ref, rows_ref, sems):
    fetch_labels = pltpu.make_async_copy(labels_hbm, labels_ref, sems.at[0])
    fetch_points = pltpu.make_async_copy(points_hbm, points_ref, sems.at[1])
    fetch_labels.start()
    fetch_points.start()
    fetch_labels.wait()
    labels = labels_ref[...]
    group = ((labels >> 7) * 171) >> 9
    local = labels - group * GROUP
    member = jnp.where(iota((N_DP, PTS), 0) == group, 1.0, 0.0)
    member16 = member.astype(bf16)
    width = 256
    n_chunks = PTS // width
    stacked = jnp.concatenate(
        [member16[:, c * width : (c + 1) * width] for c in range(n_chunks)], axis=0
    )
    before = hot(iota((width, 2 * width), 0) < iota((width, 2 * width), 1))
    prefix = dot_nn(stacked, before)
    base = jnp.zeros((N_DP, width), f32)
    ranks = []
    for c in range(n_chunks):
        part = prefix[c * N_DP : (c + 1) * N_DP]
        inside = member[:, c * width : (c + 1) * width]
        ranks.append(jnp.sum(inside * (part[:, :width] + base), axis=0, keepdims=True))
        base = base + part[:, width:]
    rank = jnp.concatenate(ranks, axis=1).astype(i32)
    r1 = rank & 7
    r2 = rank >> 3
    key = rows_of((group * 8 + r2).astype(f32), N_DP * 8)

    line = iota((N_DP, PTS), 0)
    digit = jnp.where((line & 1) == 0, local >> 3, local & 7).astype(f32)
    pair = ((group >> 2) << 1) | (group & 1)
    digit = jnp.where((line >> 1) == pair, digit, 0.0).astype(bf16)
    place = lax.axis_index("z") * 4 + lax.axis_index("xh") * 2 + lax.axis_index("core")
    slot = ((group >> 1) & 1) * 4 + (r1 & 3)
    spot = (16 * (place + slot) + (r1 >> 2) * 8 + r2) & 127

    fetch_points.wait()
    points = points_ref[...]
    masks = [hot(r1 == r) for r in range(8)]
    split = jnp.concatenate(
        [points[32 * half : 32 * half + 32] * masks[r] for half in range(2) for r in range(8)], axis=0
    )
    moved = dot_nt(key, split)
    tags = dot_nt(digit, rows_of(spot.astype(f32), 128))
    for d in range(N_DP):
        first, half = d & ~2, (d >> 1) & 1
        pair = (d >> 2) * 2 + (d & 1)
        for own in range(2):
            for h in range(2):
                at = STRIDE * d + 16 * own + 8 * h
                line, lane = 8 * (first + 2 * own), 256 * half + 128 * h
                rows_ref[at : at + 8, :] = moved[line : line + 8, lane : lane + 128]
        rows_ref[STRIDE * d + 32 : STRIDE * d + 34, :] = tags[2 * pair : 2 * pair + 2]
    out_ref[...] = rows_ref[...].astype(bf16)


def sum_kernel(parent_hbm, in_ref, out_ref, keep_ref, count_ref, parent_ref, rows_ref, sem):
    fetch = pltpu.make_async_copy(parent_hbm, parent_ref, sem)
    fetch.start()
    rows_ref[...] = in_ref[...].astype(f32)
    tags = 8.0 * rows_ref[pl.ds(32, N_DP, stride=STRIDE), :] + rows_ref[pl.ds(33, N_DP, stride=STRIDE), :]
    mine = iota((8, 128), 1) >> 4 == iota((8, 128), 0)
    quarter = iota((GROUP, 128), 1) >> 5
    half = N_DP * 16
    sides = [hot(iota((1, 128), 1) >> 5 == s) for s in range(4)]
    wides, squares = [], []
    for own in range(2):
        data = jnp.concatenate(
            [rows_ref[STRIDE * i + 16 * own : STRIDE * i + 16 * own + 16, :] for i in range(N_DP)], axis=0
        ).astype(bf16)
        labels = []
        for s in range(4):
            slot = own * 4 + s
            turned = pltpu.roll(tags, 128 - 16 * slot, 1) if slot else tags
            labels += [
                jnp.sum(jnp.where(mine, turned[8 * t : 8 * t + 8], 0.0), axis=0, keepdims=True)
                for t in range(4)
            ]
        split = jnp.concatenate([data * side for side in sides], axis=0)
        split = jnp.concatenate([split, jnp.ones((4 * half, 128), bf16)], axis=1)
        result = dot_nn(rows_of(jnp.concatenate(labels, axis=1), GROUP), split)
        sums, counts = result[:, :128], result[:, 128:]
        sums = sums + pltpu.roll(sums, 64, 1)
        sums = sums + pltpu.roll(sums, 32, 1)
        turned = jnp.where(quarter == 0, sums, counts).T
        keep_ref[:, own * GROUP : (own + 1) * GROUP] = turned[:32]
        count_ref[:, own * GROUP : (own + 1) * GROUP] = turned[32:40]
        square = jnp.sum(turned[:32] * turned[:32], axis=0, keepdims=True)
        squares += [square[:, 128 * c : 128 * (c + 1)] for c in range(3)]
        sums = sums.reshape(N_MP, 3, 8, 128)
        band = iota((N_MP, 8, 128), 2) >> 5
        wide = jnp.where(band == 0, sums[:, 0], jnp.where(band == 1, sums[:, 1], sums[:, 2]))
        wides.append(wide.astype(bf16))
    fetch.wait()
    parent = parent_ref[...]
    parent = jnp.concatenate([parent >> 3, parent & 7], axis=0).astype(f32)
    parent = jnp.concatenate([parent, jnp.zeros((2, 128 - ROWS), f32)], axis=1)
    tail = jnp.concatenate(squares + [parent], axis=0).astype(bf16)
    for own in range(2):
        block = slice(N_MP * own, N_MP * (own + 1))
        out_ref[block, 0:8, :] = wides[own]
    out_ref[:, 8:16, :] = jnp.broadcast_to(tail[None], (2 * N_MP, 8, 128))


def unit_kernel(in_ref, keep_ref, other_ref, count_ref, level2_ref, out_ref):
    band = iota((8, 128), 1) >> 5
    rows = ([], [], [])
    for c in range(N_MP // 2):
        parts = []
        for b in range(4):
            source = N_MP * (b & 1) + 2 * c + (b >> 1)
            parts.append(in_ref[source, 0:8, :].astype(f32))
        for g in range(3):
            line = None
            for b in range(4):
                part = pltpu.roll(parts[b], (32 * (b - g)) % 128, 1) if b != g else parts[b]
                line = part if line is None else jnp.where(band == b, part, line)
            rows[g].append(line)
    lines = jnp.concatenate([jnp.concatenate(r, axis=1) for r in rows], axis=0)
    scale = lax.rsqrt(jnp.sum(lines * lines, axis=1, keepdims=True) * (1.0 / D) + EPS)
    level2_ref[...] = (lines * scale).astype(bf16)

    tails = in_ref[:, 8:16, :].astype(f32)
    squares = jnp.sum(tails, axis=0)
    squares = jnp.concatenate([squares[c : c + 1] for c in range(6)], axis=1)
    scale = lax.rsqrt(squares * (1.0 / D) + EPS)
    named = 8.0 * tails[:, 6:7] + tails[:, 7:8]
    named = jnp.concatenate(
        [pltpu.roll(named[n], (ROWS * n) % 128, 1) if n % N_MP else named[n] for n in range(2 * N_MP)], axis=0
    )
    parent = []
    for c in range(6):
        place = iota((2 * N_MP, 128), 1) + 128 * c
        mine = ((place >> 3) * 171) >> 9 == iota((2 * N_MP, 128), 0)
        parent.append(jnp.sum(jnp.where(mine, named, 0.0), axis=0, keepdims=True))
    parent = jnp.concatenate(parent, axis=1).astype(i32)
    side = lax.axis_index("xl")
    line = (((parent >> 3) & 15) * 8 + (parent >> 8)) * 4 + (parent & 3)
    line = jnp.where(((parent >> 7) & 1) == side, line, -1)
    key = rows_of(line.astype(f32), N_DP * N_MP)

    factor = count_ref[0:1, :]
    own = (keep_ref[...] * scale).astype(bf16).astype(f32) * factor
    other = (other_ref[...] * scale).astype(bf16).astype(f32) * factor
    part = (parent >> 2) & 1
    both = jnp.concatenate(
        [
            jnp.where(part == s, block, 0.0)
            for block in (jnp.where(side == 0, own, other), jnp.where(side == 0, other, own))
            for s in range(2)
        ],
        axis=0,
    )
    high = both.astype(bf16)
    low = (both - high.astype(f32)).astype(bf16)
    total = dot_nt(key, jnp.concatenate([high, low], axis=0))
    out_ref[...] = (total[:, :128] + total[:, 128:]).astype(bf16)


def spread_kernel(in_ref, out_ref):
    total = jnp.sum(in_ref[...].astype(f32).reshape(N_DP // 2, 32, 128), axis=0).reshape(4, 8, 128)
    odd, lower = (iota((4, 8, 128), 2) >> 5) & 1, iota((4, 8, 128), 1) >> 2
    swapped = pltpu.roll(total, 4, 1)
    swapped = jnp.where(lower == 0, pltpu.roll(swapped, 32, 2), pltpu.roll(swapped, 96, 2))
    out = jnp.where(odd == lower, total, swapped)
    out = jnp.where(lax.axis_index("xh") == 1, pltpu.roll(out, 32, 2), out)
    out_ref[...] = jnp.broadcast_to(out.reshape(32, 128).astype(bf16)[None], (N_DP, 32, 128))


def finish_kernel(in_ref, level2_ref, out_hbm, level2_hbm, out_ref, sems):
    stores = [pltpu.make_async_copy(level2_ref, level2_hbm, sems.at[2])]
    stores[0].start()
    band = iota((N_MP, 8, 128), 2) >> 5
    places = [(p >> 1) * 4 + (p & 1) for p in range(N_DP // 2)]
    tiles = []
    square = jnp.zeros((N_MP, 8, 128), f32)
    for t in range(4):
        block = pl.ds(8 * t, 8)
        first = jnp.concatenate([in_ref[n : n + 1, block, :] for n in places], axis=0).astype(f32)
        second = jnp.concatenate([in_ref[n + 2 : n + 3, block, :] for n in places], axis=0).astype(f32)
        even = (band & 1) == 0
        tiles.append(jnp.where(even, first, second))
        tiles.append(pltpu.roll(jnp.where(even, second, first), 96, 2))
        square = square + tiles[-1] * tiles[-1] + tiles[-2] * tiles[-2]
    scale = lax.rsqrt(jnp.sum(square, axis=2, keepdims=True) * (1.0 / D) + EPS)
    for n in range(2):
        block = pl.ds(64 * n, 64)
        for c in range(8):
            part = tiles[c][8 * n : 8 * n + 8] * scale[8 * n : 8 * n + 8]
            out_ref[block, 128 * c : 128 * (c + 1)] = part.reshape(64, 128).astype(bf16)
        stores.append(pltpu.make_async_copy(out_ref.at[block], out_hbm.at[block], sems.at[n]))
        stores[-1].start()
    for store in stores:
        store.wait()


def call(kernel, out, *args, far=(), scratch=(), spaces=(pltpu.VMEM,)):
    many = isinstance(out, tuple)
    results = tuple(pl.BlockSpec(memory_space=space) for space in spaces)
    return pl.pallas_call(
        kernel,
        out_shape=out,
        in_specs=[pl.BlockSpec(memory_space=pltpu.HBM)] * len(far)
        + [pl.BlockSpec(memory_space=pltpu.VMEM)] * len(args),
        out_specs=results if many else results[0],
        scratch_shapes=scratch,
        compiler_params=pltpu.CompilerParams(vmem_limit_bytes=48 * 1024 * 1024),
    )(*(pltpu.with_memory_space_constraint(x, pltpu.HBM) for x in far), *args)


def shape(dims, dtype):
    return jax.ShapeDtypeStruct(dims, dtype)


def exchange(x, axis):
    return lax.all_to_all(x, axis, 0, 0, tiled=True)


def body(points, point_cluster, cluster_parent):
    rows = N_DP * STRIDE
    sent = call(
        sort_kernel,
        shape((rows, 128), bf16),
        far=(point_cluster.T, points.T),
        scratch=(
            pltpu.VMEM((1, PTS), i32),
            pltpu.VMEM((FEAT, PTS), bf16),
            pltpu.VMEM((rows, 128), f32),
            pltpu.SemaphoreType.DMA((2,)),
        ),
    )
    got = exchange(sent.reshape(N_DP, STRIDE // 2, 2, 128), ("z", "xh", "core")).reshape(rows, 128)
    sums, keep, counts = call(
        sum_kernel,
        (shape((2 * N_MP, 16, 128), bf16), shape((32, 2 * GROUP), f32), shape((8, 2 * GROUP), f32)),
        got,
        far=(cluster_parent.T,),
        scratch=(
            pltpu.VMEM((1, ROWS), i32),
            pltpu.VMEM((rows, 128), f32),
            pltpu.SemaphoreType.DMA(()),
        ),
        spaces=(pltpu.VMEM,) * 3,
    )
    other = lax.ppermute(keep, "xl", [(0, 1), (1, 0)])
    peers = N_DP // 2 * N_MP // 2
    level2, partial = call(
        unit_kernel,
        (shape((ROWS, D), bf16), shape((4 * peers, 128), bf16)),
        exchange(sums, ("xh", "y", "xl")),
        keep,
        other,
        counts,
        spaces=(pltpu.VMEM, pltpu.VMEM),
    )
    parts = exchange(partial.reshape(peers, 4, 128), ("z", "core", "y")).reshape(4 * peers, 128)
    parents = call(spread_kernel, shape((N_DP, 32, 128), bf16), parts)
    level3, level2 = call(
        finish_kernel,
        (shape((K3_MP, D), bf16), shape((ROWS, D), bf16)),
        exchange(parents, ("z", "xh", "core")),
        level2,
        scratch=(pltpu.VMEM((K3_MP, D), bf16), pltpu.SemaphoreType.DMA((3,))),
        spaces=(pltpu.HBM, pltpu.HBM),
    )
    return (level2, level3)


def solution(mesh):
    split = Mesh(mesh.devices.reshape(N_DP // 4, 2, 2, N_MP // 2, 2), ("z", "xh", "core", "y", "xl"))
    dp, mp = ("z", "xh", "core"), ("y", "xl")
    placed = (P(dp, mp), P(dp, None), P((*dp, *mp), None))
    return jax.shard_map(
        body,
        mesh=split,
        in_specs=placed,
        out_specs=(P((*dp, *mp), None), P(mp, None)),
        check_vma=False,
    )
```

```python
import jax
import jax.numpy as jnp
from jax import lax
from jax.experimental import pallas as pl
from jax.experimental.pallas import tpu as pltpu
from jax.sharding import Mesh
from jax.sharding import PartitionSpec as P

N_DP = 32
N_MP = 16
PTS = 2048
FEAT = 64
ROWS = 24
GROUP = ROWS * N_MP
D = 1024
K3 = 2048
K3_MP = 128
EPS = 1e-06
STRIDE = 34

f32 = jnp.float32
bf16 = jnp.bfloat16
i32 = jnp.int32


def iota(shape, dim):
    return lax.broadcasted_iota(i32, shape, dim)


def rows_of(row, n):
    one, zero = jnp.ones((), bf16), jnp.zeros((), bf16)
    blocks = []
    for at in range(0, n, 256):
        number = iota((min(256, n - at), row.shape[1]), 0).astype(f32).astype(bf16)
        blocks.append(jnp.where(number == (row - at).astype(bf16), one, zero))
    return jnp.concatenate(blocks, axis=0)


def hot(mask):
    return jnp.where(mask, 1.0, 0.0).astype(bf16)


def dot_nt(a, b):
    return lax.dot_general(a, b, (((1,), (1,)), ((), ())), preferred_element_type=f32)


def dot_nn(a, b):
    return lax.dot_general(a, b, (((1,), (0,)), ((), ())), preferred_element_type=f32)


def sort_kernel(labels_hbm, points_hbm, out_ref, labels_ref, points_ref, rows_ref, sems):
    fetch_labels = pltpu.make_async_copy(labels_hbm, labels_ref, sems.at[0])
    fetch_points = pltpu.make_async_copy(points_hbm, points_ref, sems.at[1])
    fetch_labels.start()
    fetch_points.start()
    fetch_labels.wait()
    labels = labels_ref[...]
    group = ((labels >> 7) * 171) >> 9
    local = labels - group * GROUP
    member = jnp.where(iota((N_DP, PTS), 0) == group, 1.0, 0.0)
    member16 = member.astype(bf16)
    width = 256
    n_chunks = PTS // width
    stacked = jnp.concatenate(
        [member16[:, c * width : (c + 1) * width] for c in range(n_chunks)], axis=0
    )
    before = hot(iota((width, 2 * width), 0) < iota((width, 2 * width), 1))
    prefix = dot_nn(stacked, before)
    base = jnp.zeros((N_DP, width), f32)
    ranks = []
    for c in range(n_chunks):
        part = prefix[c * N_DP : (c + 1) * N_DP]
        inside = member[:, c * width : (c + 1) * width]
        ranks.append(jnp.sum(inside * (part[:, :width] + base), axis=0, keepdims=True))
        base = base + part[:, width:]
    rank = jnp.concatenate(ranks, axis=1).astype(i32)
    r1 = rank & 7
    r2 = rank >> 3
    key = rows_of((group * 8 + r2).astype(f32), N_DP * 8)

    line = iota((N_DP, PTS), 0)
    digit = jnp.where((line & 1) == 0, local >> 3, local & 7).astype(f32)
    pair = ((group >> 2) << 1) | (group & 1)
    digit = jnp.where((line >> 1) == pair, digit, 0.0).astype(bf16)
    place = lax.axis_index("z") * 4 + lax.axis_index("xh") * 2 + lax.axis_index("core")
    slot = ((group >> 1) & 1) * 4 + (r1 & 3)
    spot = (16 * (place + slot) + (r1 >> 2) * 8 + r2) & 127

    fetch_points.wait()
    points = points_ref[...]
    masks = [hot(r1 == r) for r in range(8)]
    split = jnp.concatenate(
        [points[32 * half : 32 * half + 32] * masks[r] for half in range(2) for r in range(8)], axis=0
    )
    moved = dot_nt(key, split)
    tags = dot_nt(digit, rows_of(spot.astype(f32), 128))
    for d in range(N_DP):
        first, half = d & ~2, (d >> 1) & 1
        pair = (d >> 2) * 2 + (d & 1)
        for own in range(2):
            for h in range(2):
                at = STRIDE * d + 16 * own + 8 * h
                line, lane = 8 * (first + 2 * own), 256 * half + 128 * h
                rows_ref[at : at + 8, :] = moved[line : line + 8, lane : lane + 128]
        rows_ref[STRIDE * d + 32 : STRIDE * d + 34, :] = tags[2 * pair : 2 * pair + 2]
    out_ref[...] = rows_ref[...].astype(bf16)


def sum_kernel(parent_hbm, in_ref, out_ref, keep_ref, count_ref, parent_ref, rows_ref, sem):
    fetch = pltpu.make_async_copy(parent_hbm, parent_ref, sem)
    fetch.start()
    rows_ref[...] = in_ref[...].astype(f32)
    tags = 8.0 * rows_ref[pl.ds(32, N_DP, stride=STRIDE), :] + rows_ref[pl.ds(33, N_DP, stride=STRIDE), :]
    mine = iota((8, 128), 1) >> 4 == iota((8, 128), 0)
    quarter = iota((GROUP, 128), 1) >> 5
    half = N_DP * 16
    sides = [hot(iota((1, 128), 1) >> 5 == s) for s in range(4)]
    wides, squares = [], []
    for own in range(2):
        data = jnp.concatenate(
            [rows_ref[STRIDE * i + 16 * own : STRIDE * i + 16 * own + 16, :] for i in range(N_DP)], axis=0
        ).astype(bf16)
        labels = []
        for s in range(4):
            slot = own * 4 + s
            turned = pltpu.roll(tags, 128 - 16 * slot, 1) if slot else tags
            labels += [
                jnp.sum(jnp.where(mine, turned[8 * t : 8 * t + 8], 0.0), axis=0, keepdims=True)
                for t in range(4)
            ]
        split = jnp.concatenate([data * side for side in sides], axis=0)
        split = jnp.concatenate([split, jnp.ones((4 * half, 128), bf16)], axis=1)
        result = dot_nn(rows_of(jnp.concatenate(labels, axis=1), GROUP), split)
        sums, counts = result[:, :128], result[:, 128:]
        sums = sums + pltpu.roll(sums, 64, 1)
        sums = sums + pltpu.roll(sums, 32, 1)
        turned = jnp.where(quarter == 0, sums, counts).T
        keep_ref[:, own * GROUP : (own + 1) * GROUP] = turned[:32]
        count_ref[:, own * GROUP : (own + 1) * GROUP] = turned[32:40]
        square = jnp.sum(turned[:32] * turned[:32], axis=0, keepdims=True)
        squares += [square[:, 128 * c : 128 * (c + 1)] for c in range(3)]
        sums = sums.reshape(N_MP, 3, 8, 128)
        band = iota((N_MP, 8, 128), 2) >> 5
        wide = jnp.where(band == 0, sums[:, 0], jnp.where(band == 1, sums[:, 1], sums[:, 2]))
        wides.append(wide.astype(bf16))
    fetch.wait()
    parent = parent_ref[...]
    parent = jnp.concatenate([parent >> 3, parent & 7], axis=0).astype(f32)
    parent = jnp.concatenate([parent, jnp.zeros((2, 128 - ROWS), f32)], axis=1)
    tail = jnp.concatenate(squares + [parent], axis=0).astype(bf16)
    for own in range(2):
        block = slice(N_MP * own, N_MP * (own + 1))
        out_ref[block, 0:8, :] = wides[own]
    out_ref[:, 8:16, :] = jnp.broadcast_to(tail[None], (2 * N_MP, 8, 128))


def unit_kernel(in_ref, keep_ref, count_ref, level2_ref, out_ref):
    band = iota((8, 128), 1) >> 5
    rows = ([], [], [])
    for c in range(N_MP // 2):
        parts = []
        for b in range(4):
            source = N_MP * (b & 1) + 2 * c + (b >> 1)
            parts.append(in_ref[source, 0:8, :].astype(f32))
        for g in range(3):
            line = None
            for b in range(4):
                part = pltpu.roll(parts[b], (32 * (b - g)) % 128, 1) if b != g else parts[b]
                line = part if line is None else jnp.where(band == b, part, line)
            rows[g].append(line)
    lines = jnp.concatenate([jnp.concatenate(r, axis=1) for r in rows], axis=0)
    scale = lax.rsqrt(jnp.sum(lines * lines, axis=1, keepdims=True) * (1.0 / D) + EPS)
    level2_ref[...] = (lines * scale).astype(bf16)

    tails = in_ref[:, 8:16, :].astype(f32)
    squares = jnp.sum(tails, axis=0)
    squares = jnp.concatenate([squares[c : c + 1] for c in range(6)], axis=1)
    scale = lax.rsqrt(squares * (1.0 / D) + EPS)
    named = 8.0 * tails[:, 6:7] + tails[:, 7:8]
    named = jnp.concatenate(
        [pltpu.roll(named[n], (ROWS * n) % 128, 1) if n % N_MP else named[n] for n in range(2 * N_MP)], axis=0
    )
    parent = []
    for c in range(6):
        place = iota((2 * N_MP, 128), 1) + 128 * c
        mine = ((place >> 3) * 171) >> 9 == iota((2 * N_MP, 128), 0)
        parent.append(jnp.sum(jnp.where(mine, named, 0.0), axis=0, keepdims=True))
    parent = jnp.concatenate(parent, axis=1).astype(i32)
    line = (((parent >> 3) & 15) * 8 + (parent >> 8)) * 4 + ((parent >> 7) & 1) * 2 + (parent & 1)
    key = rows_of(line.astype(f32), N_DP * N_MP)

    weighted = (keep_ref[...] * scale).astype(bf16).astype(f32) * count_ref[0:1, :]
    part = (parent >> 1) & 3
    both = jnp.concatenate([jnp.where(part == s, weighted, 0.0) for s in range(4)], axis=0)
    high = both.astype(bf16)
    low = (both - high.astype(f32)).astype(bf16)
    total = dot_nt(key, jnp.concatenate([high, low], axis=0))
    out_ref[...] = (total[:, :128] + total[:, 128:]).astype(bf16)


def spread_kernel(in_ref, out_ref):
    total = jnp.sum(in_ref[...].astype(f32).reshape(N_DP // 2, 32, 128), axis=0).reshape(4, 8, 128)
    band, part = iota((2, 8, 128), 2) >> 5, iota((2, 8, 128), 1) >> 1
    even = jnp.concatenate([total[0:1], total[2:3]], axis=0)
    odd = jnp.concatenate([total[1:2], total[3:4]], axis=0)
    pieces = []
    for xl in range(2):
        out = jnp.zeros((2, 8, 128), f32)
        for y in range(4):
            for s in range(4):
                piece = odd if y >> 1 else even
                across, down = (32 * (y - s)) % 128, (2 * s - 4 * (y & 1) - 2 * xl) % 8
                piece = pltpu.roll(piece, across, 2) if across else piece
                piece = pltpu.roll(piece, down, 1) if down else piece
                out = jnp.where((band == y) & (part == s), piece, out)
        pieces.append(out)
    out = jnp.concatenate(pieces, axis=0)
    place = 2 * lax.axis_index("xl") + lax.axis_index("xh")
    turned = out
    for n in range(1, 4):
        turned = jnp.where(place == n, pltpu.roll(out, 32 * n, 2), turned)
    out_ref[...] = jnp.broadcast_to(turned.reshape(32, 128).astype(bf16)[None], (N_DP, 32, 128))


def finish_kernel(in_ref, level2_ref, out_hbm, level2_hbm, out_ref, sems):
    stores = [pltpu.make_async_copy(level2_ref, level2_hbm, sems.at[2])]
    stores[0].start()
    band = iota((N_DP // 2, 8, 128), 2) >> 5
    places = [(p >> 1) * 4 + (p & 1) for p in range(N_DP // 2)]
    tiles = []
    square = jnp.zeros((N_DP // 2, 8, 128), f32)
    for t in range(2):
        block = pl.ds(8 * t, 8)
        parts = []
        for n in range(4):
            source = [2 * (place + 2 * (n & 1)) + (n >> 1) for place in places]
            parts.append(jnp.concatenate([in_ref[m : m + 1, block, :] for m in source], axis=0).astype(f32))
        for y in range(4):
            tile = parts[0]
            for n in range(1, 4):
                tile = jnp.where(band == (y + n) % 4, parts[n], tile)
            tile = pltpu.roll(tile, 128 - 32 * y, 2) if y else tile
            tiles.append(tile)
            square = square + tile * tile
    scale = lax.rsqrt(jnp.sum(square, axis=2, keepdims=True) * (1.0 / D) + EPS)
    for n in range(2):
        block = pl.ds(64 * n, 64)
        for c in range(8):
            part = tiles[c][8 * n : 8 * n + 8] * scale[8 * n : 8 * n + 8]
            out_ref[block, 128 * c : 128 * (c + 1)] = part.reshape(64, 128).astype(bf16)
        stores.append(pltpu.make_async_copy(out_ref.at[block], out_hbm.at[block], sems.at[n]))
        stores[-1].start()
    for store in stores:
        store.wait()


def call(kernel, out, *args, far=(), scratch=(), spaces=(pltpu.VMEM,)):
    many = isinstance(out, tuple)
    results = tuple(pl.BlockSpec(memory_space=space) for space in spaces)
    return pl.pallas_call(
        kernel,
        out_shape=out,
        in_specs=[pl.BlockSpec(memory_space=pltpu.HBM)] * len(far)
        + [pl.BlockSpec(memory_space=pltpu.VMEM)] * len(args),
        out_specs=results if many else results[0],
        scratch_shapes=scratch,
        compiler_params=pltpu.CompilerParams(vmem_limit_bytes=48 * 1024 * 1024),
    )(*(pltpu.with_memory_space_constraint(x, pltpu.HBM) for x in far), *args)


def shape(dims, dtype):
    return jax.ShapeDtypeStruct(dims, dtype)


def exchange(x, axis):
    return lax.all_to_all(x, axis, 0, 0, tiled=True)


def body(points, point_cluster, cluster_parent):
    rows = N_DP * STRIDE
    sent = call(
        sort_kernel,
        shape((rows, 128), bf16),
        far=(point_cluster.T, points.T),
        scratch=(
            pltpu.VMEM((1, PTS), i32),
            pltpu.VMEM((FEAT, PTS), bf16),
            pltpu.VMEM((rows, 128), f32),
            pltpu.SemaphoreType.DMA((2,)),
        ),
    )
    got = exchange(sent.reshape(N_DP, STRIDE // 2, 2, 128), ("z", "xh", "core")).reshape(rows, 128)
    sums, keep, counts = call(
        sum_kernel,
        (shape((2 * N_MP, 16, 128), bf16), shape((32, 2 * GROUP), f32), shape((8, 2 * GROUP), f32)),
        got,
        far=(cluster_parent.T,),
        scratch=(
            pltpu.VMEM((1, ROWS), i32),
            pltpu.VMEM((rows, 128), f32),
            pltpu.SemaphoreType.DMA(()),
        ),
        spaces=(pltpu.VMEM,) * 3,
    )
    peers = N_DP // 2 * N_MP // 2
    level2, partial = call(
        unit_kernel,
        (shape((ROWS, D), bf16), shape((4 * peers, 128), bf16)),
        exchange(sums, ("xh", "y", "xl")),
        keep,
        counts,
        spaces=(pltpu.VMEM, pltpu.VMEM),
    )
    parts = exchange(partial.reshape(peers, 4, 128), ("z", "core", "y")).reshape(4 * peers, 128)
    parents = call(spread_kernel, shape((N_DP, 32, 128), bf16), parts)
    level3, level2 = call(
        finish_kernel,
        (shape((K3_MP, D), bf16), shape((ROWS, D), bf16)),
        exchange(parents.reshape(2 * N_DP, 16, 128), ("z", "xh", "core", "xl")),
        level2,
        scratch=(pltpu.VMEM((K3_MP, D), bf16), pltpu.SemaphoreType.DMA((3,))),
        spaces=(pltpu.HBM, pltpu.HBM),
    )
    return (level2, level3)


def solution(mesh):
    split = Mesh(mesh.devices.reshape(N_DP // 4, 2, 2, N_MP // 2, 2), ("z", "xh", "core", "y", "xl"))
    dp, mp = ("z", "xh", "core"), ("y", "xl")
    placed = (P(dp, mp), P(dp, None), P((*dp, *mp), None))
    return jax.shard_map(
        body,
        mesh=split,
        in_specs=placed,
        out_specs=(P((*dp, *mp), None), P(mp, None)),
        check_vma=False,
    )
```

```python
import jax
import jax.numpy as jnp
from jax import lax
from jax.experimental import pallas as pl
from jax.experimental.pallas import tpu as pltpu
from jax.sharding import Mesh
from jax.sharding import PartitionSpec as P

N_DP = 32
N_MP = 16
PTS = 2048
FEAT = 64
ROWS = 24
GROUP = ROWS * N_MP
D = 1024
K3 = 2048
K3_MP = 128
EPS = 1e-06
STRIDE = 34

f32 = jnp.float32
bf16 = jnp.bfloat16
i32 = jnp.int32


def iota(shape, dim):
    return lax.broadcasted_iota(i32, shape, dim)


def rows_of(row, n):
    one, zero = jnp.ones((), bf16), jnp.zeros((), bf16)
    blocks = []
    for at in range(0, n, 256):
        number = iota((min(256, n - at), row.shape[1]), 0).astype(f32).astype(bf16)
        blocks.append(jnp.where(number == (row - at).astype(bf16), one, zero))
    return jnp.concatenate(blocks, axis=0)


def hot(mask):
    return jnp.where(mask, 1.0, 0.0).astype(bf16)


def dot_nt(a, b):
    return lax.dot_general(a, b, (((1,), (1,)), ((), ())), preferred_element_type=f32)


def dot_nn(a, b):
    return lax.dot_general(a, b, (((1,), (0,)), ((), ())), preferred_element_type=f32)


def sort_kernel(labels_hbm, points_hbm, out_ref, labels_ref, points_ref, rows_ref, sems):
    fetch_labels = pltpu.make_async_copy(labels_hbm, labels_ref, sems.at[0])
    fetch_points = pltpu.make_async_copy(points_hbm, points_ref, sems.at[1])
    fetch_labels.start()
    fetch_points.start()
    fetch_labels.wait()
    labels = labels_ref[...]
    group = ((labels >> 7) * 171) >> 9
    local = labels - group * GROUP
    member = jnp.where(iota((N_DP, PTS), 0) == group, 1.0, 0.0)
    member16 = member.astype(bf16)
    width = 256
    n_chunks = PTS // width
    stacked = jnp.concatenate(
        [member16[:, c * width : (c + 1) * width] for c in range(n_chunks)], axis=0
    )
    before = hot(iota((width, 2 * width), 0) < iota((width, 2 * width), 1))
    prefix = dot_nn(stacked, before)
    base = jnp.zeros((N_DP, width), f32)
    ranks = []
    for c in range(n_chunks):
        part = prefix[c * N_DP : (c + 1) * N_DP]
        inside = member[:, c * width : (c + 1) * width]
        ranks.append(jnp.sum(inside * (part[:, :width] + base), axis=0, keepdims=True))
        base = base + part[:, width:]
    rank = jnp.concatenate(ranks, axis=1).astype(i32)
    r1 = rank & 7
    r2 = rank >> 3
    key = rows_of((group * 8 + r2).astype(f32), N_DP * 8)

    line = iota((N_DP, PTS), 0)
    digit = jnp.where((line & 1) == 0, local >> 3, local & 7).astype(f32)
    pair = ((group >> 2) << 1) | (group & 1)
    digit = jnp.where((line >> 1) == pair, digit, 0.0).astype(bf16)
    place = lax.axis_index("z") * 4 + lax.axis_index("xh") * 2 + lax.axis_index("core")
    slot = ((group >> 1) & 1) * 4 + (r1 & 3)
    spot = (16 * (place + slot) + (r1 >> 2) * 8 + r2) & 127

    fetch_points.wait()
    points = points_ref[...]
    masks = [hot(r1 == r) for r in range(8)]
    split = jnp.concatenate(
        [points[32 * half : 32 * half + 32] * masks[r] for half in range(2) for r in range(8)], axis=0
    )
    moved = dot_nt(key, split)
    tags = dot_nt(digit, rows_of(spot.astype(f32), 128))
    for d in range(N_DP):
        first, half = d & ~2, (d >> 1) & 1
        pair = (d >> 2) * 2 + (d & 1)
        for own in range(2):
            for h in range(2):
                at = STRIDE * d + 16 * own + 8 * h
                line, lane = 8 * (first + 2 * own), 256 * half + 128 * h
                rows_ref[at : at + 8, :] = moved[line : line + 8, lane : lane + 128]
        rows_ref[STRIDE * d + 32 : STRIDE * d + 34, :] = tags[2 * pair : 2 * pair + 2]
    out_ref[...] = rows_ref[...].astype(bf16)


def sum_kernel(parent_hbm, in_ref, out_ref, keep_ref, count_ref, parent_ref, rows_ref, sem):
    fetch = pltpu.make_async_copy(parent_hbm, parent_ref, sem)
    fetch.start()
    rows_ref[...] = in_ref[...].astype(f32)
    tags = 8.0 * rows_ref[pl.ds(32, N_DP, stride=STRIDE), :] + rows_ref[pl.ds(33, N_DP, stride=STRIDE), :]
    mine = iota((8, 128), 1) >> 4 == iota((8, 128), 0)
    quarter = iota((GROUP, 128), 1) >> 5
    half = N_DP * 16
    sides = [hot(iota((1, 128), 1) >> 5 == s) for s in range(4)]
    wides, squares = [], []
    for own in range(2):
        data = jnp.concatenate(
            [rows_ref[STRIDE * i + 16 * own : STRIDE * i + 16 * own + 16, :] for i in range(N_DP)], axis=0
        ).astype(bf16)
        labels = []
        for s in range(4):
            slot = own * 4 + s
            turned = pltpu.roll(tags, 128 - 16 * slot, 1) if slot else tags
            labels += [
                jnp.sum(jnp.where(mine, turned[8 * t : 8 * t + 8], 0.0), axis=0, keepdims=True)
                for t in range(4)
            ]
        split = jnp.concatenate([data * side for side in sides], axis=0)
        split = jnp.concatenate([split, jnp.ones((4 * half, 128), bf16)], axis=1)
        result = dot_nn(rows_of(jnp.concatenate(labels, axis=1), GROUP), split)
        sums, counts = result[:, :128], result[:, 128:]
        sums = sums + pltpu.roll(sums, 64, 1)
        sums = sums + pltpu.roll(sums, 32, 1)
        turned = jnp.where(quarter == 0, sums, counts).T
        keep_ref[:, own * GROUP : (own + 1) * GROUP] = turned[:32]
        count_ref[:, own * GROUP : (own + 1) * GROUP] = turned[32:40]
        square = jnp.sum(turned[:32] * turned[:32], axis=0, keepdims=True)
        squares += [square[:, 128 * c : 128 * (c + 1)] for c in range(3)]
        sums = sums.reshape(N_MP, 3, 8, 128)
        band = iota((N_MP, 8, 128), 2) >> 5
        wide = jnp.where(band == 0, sums[:, 0], jnp.where(band == 1, sums[:, 1], sums[:, 2]))
        wides.append(wide.astype(bf16))
    fetch.wait()
    parent = parent_ref[...]
    parent = jnp.concatenate([parent >> 3, parent & 7], axis=0).astype(f32)
    parent = jnp.concatenate([parent, jnp.zeros((2, 128 - ROWS), f32)], axis=1)
    tail = jnp.concatenate(squares + [parent], axis=0).astype(bf16)
    wides = [wide.reshape(N_MP // 2, 1, 2, 8, 128) for wide in wides]
    out_ref[:, 0:8, :] = jnp.concatenate(wides, axis=1).reshape(2 * N_MP, 8, 128)
    out_ref[:, 8:16, :] = jnp.broadcast_to(tail[None], (2 * N_MP, 8, 128))


def unit_kernel(in_ref, keep_ref, count_ref, level2_ref, out_ref):
    band = iota((8, 128), 1) >> 5
    rows = ([], [], [])
    for c in range(N_MP // 2):
        parts = []
        for b in range(4):
            source = 4 * c + 2 * (b & 1) + (b >> 1)
            parts.append(in_ref[source, 0:8, :].astype(f32))
        for g in range(3):
            line = None
            for b in range(4):
                part = pltpu.roll(parts[b], (32 * (b - g)) % 128, 1) if b != g else parts[b]
                line = part if line is None else jnp.where(band == b, part, line)
            rows[g].append(line)
    lines = jnp.concatenate([jnp.concatenate(r, axis=1) for r in rows], axis=0)
    scale = lax.rsqrt(jnp.sum(lines * lines, axis=1, keepdims=True) * (1.0 / D) + EPS)
    level2_ref[...] = (lines * scale).astype(bf16)

    tails = in_ref[:, 8:16, :].astype(f32)
    squares = jnp.sum(tails, axis=0)
    squares = jnp.concatenate([squares[c : c + 1] for c in range(6)], axis=1)
    scale = lax.rsqrt(squares * (1.0 / D) + EPS)
    named = 8.0 * tails[:, 6:7] + tails[:, 7:8]
    order = [4 * (n % N_MP >> 1) + 2 * (n // N_MP) + (n & 1) for n in range(2 * N_MP)]
    named = jnp.concatenate(
        [
            pltpu.roll(named[m], (ROWS * n) % 128, 1) if n % N_MP else named[m]
            for n, m in enumerate(order)
        ],
        axis=0,
    )
    parent = []
    for c in range(6):
        place = iota((2 * N_MP, 128), 1) + 128 * c
        mine = ((place >> 3) * 171) >> 9 == iota((2 * N_MP, 128), 0)
        parent.append(jnp.sum(jnp.where(mine, named, 0.0), axis=0, keepdims=True))
    parent = jnp.concatenate(parent, axis=1).astype(i32)
    device = (parent >> 8) * 16 + ((parent >> 3) & 1) * 8 + ((parent >> 4) & 7)
    line = device * 4 + ((parent >> 7) & 1) * 2 + (parent & 1)
    key = rows_of(line.astype(f32), N_DP * N_MP)

    weighted = (keep_ref[...] * scale).astype(bf16).astype(f32) * count_ref[0:1, :]
    part = (parent >> 1) & 3
    both = jnp.concatenate([jnp.where(part == s, weighted, 0.0) for s in range(4)], axis=0)
    high = both.astype(bf16)
    low = (both - high.astype(f32)).astype(bf16)
    total = dot_nt(key, jnp.concatenate([high, low], axis=0))
    out_ref[...] = (total[:, :128] + total[:, 128:]).astype(bf16)


def spread_kernel(in_ref, out_ref):
    total = jnp.sum(in_ref[...].astype(f32).reshape(8, 8, 8, 128), axis=1)
    total = total + pltpu.roll(total, 4, 1)
    total = total.reshape(4, 2, 8, 128)
    total = jnp.where(iota((4, 8, 128), 1) < 4, total[:, 0], total[:, 1])
    band, part = iota((2, 8, 128), 2) >> 5, iota((2, 8, 128), 1) >> 1
    even = jnp.concatenate([total[0:1], total[2:3]], axis=0)
    odd = jnp.concatenate([total[1:2], total[3:4]], axis=0)
    pieces = []
    for xl in range(2):
        out = jnp.zeros((2, 8, 128), f32)
        for y in range(4):
            for s in range(4):
                piece = odd if y >> 1 else even
                across, down = (32 * (y - s)) % 128, (2 * s - 4 * (y & 1) - 2 * xl) % 8
                piece = pltpu.roll(piece, across, 2) if across else piece
                piece = pltpu.roll(piece, down, 1) if down else piece
                out = jnp.where((band == y) & (part == s), piece, out)
        pieces.append(out)
    out = jnp.concatenate(pieces, axis=0)
    place = 2 * lax.axis_index("xl") + lax.axis_index("xh")
    turned = out
    for n in range(1, 4):
        turned = jnp.where(place == n, pltpu.roll(out, 32 * n, 2), turned)
    out_ref[...] = jnp.broadcast_to(turned.reshape(32, 128).astype(bf16)[None], (N_DP, 32, 128))


def finish_kernel(in_ref, level2_ref, out_hbm, level2_hbm, out_ref, sems):
    stores = [pltpu.make_async_copy(level2_ref, level2_hbm, sems.at[2])]
    stores[0].start()
    band = iota((N_DP // 2, 8, 128), 2) >> 5
    places = [(p >> 1) * 4 + (p & 1) for p in range(N_DP // 2)]
    tiles = []
    square = jnp.zeros((N_DP // 2, 8, 128), f32)
    for t in range(2):
        block = pl.ds(8 * t, 8)
        parts = []
        for n in range(4):
            source = [2 * (place + 2 * (n & 1)) + (n >> 1) for place in places]
            parts.append(jnp.concatenate([in_ref[m : m + 1, block, :] for m in source], axis=0).astype(f32))
        for y in range(4):
            tile = parts[0]
            for n in range(1, 4):
                tile = jnp.where(band == (y + n) % 4, parts[n], tile)
            tile = pltpu.roll(tile, 128 - 32 * y, 2) if y else tile
            tiles.append(tile)
            square = square + tile * tile
    scale = lax.rsqrt(jnp.sum(square, axis=2, keepdims=True) * (1.0 / D) + EPS)
    for n in range(2):
        block = pl.ds(64 * n, 64)
        for c in range(8):
            part = tiles[c][8 * n : 8 * n + 8] * scale[8 * n : 8 * n + 8]
            out_ref[block, 128 * c : 128 * (c + 1)] = part.reshape(64, 128).astype(bf16)
        stores.append(pltpu.make_async_copy(out_ref.at[block], out_hbm.at[block], sems.at[n]))
        stores[-1].start()
    for store in stores:
        store.wait()


def call(kernel, out, *args, far=(), scratch=(), spaces=(pltpu.VMEM,)):
    many = isinstance(out, tuple)
    results = tuple(pl.BlockSpec(memory_space=space) for space in spaces)
    return pl.pallas_call(
        kernel,
        out_shape=out,
        in_specs=[pl.BlockSpec(memory_space=pltpu.HBM)] * len(far)
        + [pl.BlockSpec(memory_space=pltpu.VMEM)] * len(args),
        out_specs=results if many else results[0],
        scratch_shapes=scratch,
        compiler_params=pltpu.CompilerParams(vmem_limit_bytes=48 * 1024 * 1024),
    )(*(pltpu.with_memory_space_constraint(x, pltpu.HBM) for x in far), *args)


def shape(dims, dtype):
    return jax.ShapeDtypeStruct(dims, dtype)


def exchange(x, axis):
    return lax.all_to_all(x, axis, 0, 0, tiled=True)


def body(points, point_cluster, cluster_parent):
    rows = N_DP * STRIDE
    sent = call(
        sort_kernel,
        shape((rows, 128), bf16),
        far=(point_cluster.T, points.T),
        scratch=(
            pltpu.VMEM((1, PTS), i32),
            pltpu.VMEM((FEAT, PTS), bf16),
            pltpu.VMEM((rows, 128), f32),
            pltpu.SemaphoreType.DMA((2,)),
        ),
    )
    got = exchange(sent.reshape(N_DP, STRIDE // 2, 2, 128), ("z", "xh", "core")).reshape(rows, 128)
    sums, keep, counts = call(
        sum_kernel,
        (shape((2 * N_MP, 16, 128), bf16), shape((32, 2 * GROUP), f32), shape((8, 2 * GROUP), f32)),
        got,
        far=(cluster_parent.T,),
        scratch=(
            pltpu.VMEM((1, ROWS), i32),
            pltpu.VMEM((rows, 128), f32),
            pltpu.SemaphoreType.DMA(()),
        ),
        spaces=(pltpu.VMEM,) * 3,
    )
    peers = N_DP // 2 * N_MP // 2
    level2, partial = call(
        unit_kernel,
        (shape((ROWS, D), bf16), shape((4 * peers, 128), bf16)),
        exchange(sums, ("y", "xh", "xl")),
        keep,
        counts,
        spaces=(pltpu.VMEM, pltpu.VMEM),
    )
    parts = exchange(partial.reshape(peers, 4, 128), ("y", "core", "z")).reshape(4 * peers, 128)
    parents = call(spread_kernel, shape((N_DP, 32, 128), bf16), parts)
    level3, level2 = call(
        finish_kernel,
        (shape((K3_MP, D), bf16), shape((ROWS, D), bf16)),
        exchange(parents.reshape(2 * N_DP, 16, 128), ("z", "xh", "core", "xl")),
        level2,
        scratch=(pltpu.VMEM((K3_MP, D), bf16), pltpu.SemaphoreType.DMA((3,))),
        spaces=(pltpu.HBM, pltpu.HBM),
    )
    return (level2, level3)


def solution(mesh):
    split = Mesh(mesh.devices.reshape(N_DP // 4, 2, 2, N_MP // 2, 2), ("z", "xh", "core", "y", "xl"))
    dp, mp = ("z", "xh", "core"), ("y", "xl")
    placed = (P(dp, mp), P(dp, None), P((*dp, *mp), None))
    return jax.shard_map(
        body,
        mesh=split,
        in_specs=placed,
        out_specs=(P((*dp, *mp), None), P(mp, None)),
        check_vma=False,
    )
```

```python
import jax
import jax.numpy as jnp
from jax import lax
from jax.experimental import pallas as pl
from jax.experimental.pallas import tpu as pltpu
from jax.sharding import Mesh
from jax.sharding import PartitionSpec as P

N_DP = 32
N_MP = 16
PTS = 2048
FEAT = 64
ROWS = 24
GROUP = ROWS * N_MP
D = 1024
K3 = 2048
K3_MP = 128
EPS = 1e-06
STRIDE = 34

f32 = jnp.float32
bf16 = jnp.bfloat16
i32 = jnp.int32


def iota(shape, dim):
    return lax.broadcasted_iota(i32, shape, dim)


def rows_of(row, n):
    one, zero = jnp.ones((), bf16), jnp.zeros((), bf16)
    blocks = []
    for at in range(0, n, 256):
        number = iota((min(256, n - at), row.shape[1]), 0).astype(f32).astype(bf16)
        blocks.append(jnp.where(number == (row - at).astype(bf16), one, zero))
    return jnp.concatenate(blocks, axis=0)


def hot(mask):
    return jnp.where(mask, 1.0, 0.0).astype(bf16)


def dot_nt(a, b):
    return lax.dot_general(a, b, (((1,), (1,)), ((), ())), preferred_element_type=f32)


def dot_nn(a, b):
    return lax.dot_general(a, b, (((1,), (0,)), ((), ())), preferred_element_type=f32)


def sort_kernel(labels_hbm, points_hbm, out_ref, labels_ref, points_ref, rows_ref, sems):
    fetch_labels = pltpu.make_async_copy(labels_hbm, labels_ref, sems.at[0])
    fetch_points = pltpu.make_async_copy(points_hbm, points_ref, sems.at[1])
    fetch_labels.start()
    fetch_points.start()
    fetch_labels.wait()
    labels = labels_ref[...]
    group = ((labels >> 7) * 171) >> 9
    local = labels - group * GROUP
    member = jnp.where(iota((N_DP, PTS), 0) == group, 1.0, 0.0)
    member16 = member.astype(bf16)
    width = 256
    n_chunks = PTS // width
    stacked = jnp.concatenate(
        [member16[:, c * width : (c + 1) * width] for c in range(n_chunks)], axis=0
    )
    before = hot(iota((width, 2 * width), 0) < iota((width, 2 * width), 1))
    prefix = dot_nn(stacked, before)
    base = jnp.zeros((N_DP, width), f32)
    ranks = []
    for c in range(n_chunks):
        part = prefix[c * N_DP : (c + 1) * N_DP]
        inside = member[:, c * width : (c + 1) * width]
        ranks.append(jnp.sum(inside * (part[:, :width] + base), axis=0, keepdims=True))
        base = base + part[:, width:]
    rank = jnp.concatenate(ranks, axis=1).astype(i32)
    r1 = rank & 7
    r2 = rank >> 3
    key = rows_of((group * 8 + r2).astype(f32), N_DP * 8)

    line = iota((N_DP, PTS), 0)
    digit = jnp.where((line & 1) == 0, local >> 3, local & 7).astype(f32)
    pair = ((group >> 2) << 1) | (group & 1)
    digit = jnp.where((line >> 1) == pair, digit, 0.0).astype(bf16)
    place = lax.axis_index("z") * 4 + lax.axis_index("xh") * 2 + lax.axis_index("core")
    slot = ((group >> 1) & 1) * 4 + (r1 & 3)
    spot = (16 * (place + slot) + (r1 >> 2) * 8 + r2) & 127

    fetch_points.wait()
    points = points_ref[...]
    masks = [hot(r1 == r) for r in range(8)]
    split = jnp.concatenate(
        [points[32 * half : 32 * half + 32] * masks[r] for half in range(2) for r in range(8)], axis=0
    )
    moved = dot_nt(key, split)
    tags = dot_nt(digit, rows_of(spot.astype(f32), 128))
    for d in range(N_DP):
        first, half = d & ~2, (d >> 1) & 1
        pair = (d >> 2) * 2 + (d & 1)
        for own in range(2):
            for h in range(2):
                at = STRIDE * d + 16 * own + 8 * h
                line, lane = 8 * (first + 2 * own), 256 * half + 128 * h
                rows_ref[at : at + 8, :] = moved[line : line + 8, lane : lane + 128]
        rows_ref[STRIDE * d + 32 : STRIDE * d + 34, :] = tags[2 * pair : 2 * pair + 2]
    out_ref[...] = rows_ref[...].astype(bf16)


def sum_kernel(parent_hbm, in_ref, out_ref, keep_ref, count_ref, parent_ref, rows_ref, sem):
    fetch = pltpu.make_async_copy(parent_hbm, parent_ref, sem)
    fetch.start()
    rows_ref[...] = in_ref[...].astype(f32)
    tags = 8.0 * rows_ref[pl.ds(32, N_DP, stride=STRIDE), :] + rows_ref[pl.ds(33, N_DP, stride=STRIDE), :]
    mine = iota((8, 128), 1) >> 4 == iota((8, 128), 0)
    quarter = iota((GROUP, 128), 1) >> 5
    half = N_DP * 16
    sides = [hot(iota((1, 128), 1) >> 5 == s) for s in range(4)]
    wides, squares = [], []
    for own in range(2):
        data = jnp.concatenate(
            [rows_ref[STRIDE * i + 16 * own : STRIDE * i + 16 * own + 16, :] for i in range(N_DP)], axis=0
        ).astype(bf16)
        labels = []
        for s in range(4):
            slot = own * 4 + s
            turned = pltpu.roll(tags, 128 - 16 * slot, 1) if slot else tags
            labels += [
                jnp.sum(jnp.where(mine, turned[8 * t : 8 * t + 8], 0.0), axis=0, keepdims=True)
                for t in range(4)
            ]
        split = jnp.concatenate([data * side for side in sides], axis=0)
        split = jnp.concatenate([split, jnp.ones((4 * half, 128), bf16)], axis=1)
        result = dot_nn(rows_of(jnp.concatenate(labels, axis=1), GROUP), split)
        sums, counts = result[:, :128], result[:, 128:]
        sums = sums + pltpu.roll(sums, 64, 1)
        sums = sums + pltpu.roll(sums, 32, 1)
        turned = jnp.where(quarter == 0, sums, counts).T
        keep_ref[:, own * GROUP : (own + 1) * GROUP] = turned[:32]
        count_ref[:, own * GROUP : (own + 1) * GROUP] = turned[32:40]
        square = jnp.sum(turned[:32] * turned[:32], axis=0, keepdims=True)
        squares += [square[:, 128 * c : 128 * (c + 1)] for c in range(3)]
        sums = sums.reshape(N_MP, 3, 8, 128)
        band = iota((N_MP, 8, 128), 2) >> 5
        wide = jnp.where(band == 0, sums[:, 0], jnp.where(band == 1, sums[:, 1], sums[:, 2]))
        wides.append(wide.astype(bf16))
    fetch.wait()
    parent = parent_ref[...]
    parent = jnp.concatenate([parent >> 3, parent & 7], axis=0).astype(f32)
    parent = jnp.concatenate([parent, jnp.zeros((2, 128 - ROWS), f32)], axis=1)
    tail = jnp.concatenate(squares + [parent], axis=0).astype(bf16)
    wides = [wide.reshape(N_MP // 2, 1, 2, 8, 128) for wide in wides]
    out_ref[:, 0:8, :] = jnp.concatenate(wides, axis=1).reshape(2 * N_MP, 8, 128)
    out_ref[:, 8:16, :] = jnp.broadcast_to(tail[None], (2 * N_MP, 8, 128))


def unit_kernel(in_ref, keep_ref, count_ref, level2_ref, out_ref):
    band = iota((8, 128), 1) >> 5
    rows = ([], [], [])
    for c in range(N_MP // 2):
        parts = []
        for b in range(4):
            source = 4 * c + 2 * (b & 1) + (b >> 1)
            parts.append(in_ref[source, 0:8, :].astype(f32))
        for g in range(3):
            line = None
            for b in range(4):
                part = pltpu.roll(parts[b], (32 * (b - g)) % 128, 1) if b != g else parts[b]
                line = part if line is None else jnp.where(band == b, part, line)
            rows[g].append(line)
    lines = jnp.concatenate([jnp.concatenate(r, axis=1) for r in rows], axis=0)
    scale = lax.rsqrt(jnp.sum(lines * lines, axis=1, keepdims=True) * (1.0 / D) + EPS)
    level2_ref[...] = (lines * scale).astype(bf16)

    tails = in_ref[:, 8:16, :].astype(f32)
    squares = jnp.sum(tails, axis=0)
    squares = jnp.concatenate([squares[c : c + 1] for c in range(6)], axis=1)
    scale = lax.rsqrt(squares * (1.0 / D) + EPS)
    named = 8.0 * tails[:, 6:7] + tails[:, 7:8]
    order = [4 * (n % N_MP >> 1) + 2 * (n // N_MP) + (n & 1) for n in range(2 * N_MP)]
    named = jnp.concatenate(
        [
            pltpu.roll(named[m], (ROWS * n) % 128, 1) if n % N_MP else named[m]
            for n, m in enumerate(order)
        ],
        axis=0,
    )
    parent = []
    for c in range(6):
        place = iota((2 * N_MP, 128), 1) + 128 * c
        mine = ((place >> 3) * 171) >> 9 == iota((2 * N_MP, 128), 0)
        parent.append(jnp.sum(jnp.where(mine, named, 0.0), axis=0, keepdims=True))
    parent = jnp.concatenate(parent, axis=1).astype(i32)
    line = (((parent >> 3) & 15) * 8 + (parent >> 8)) * 4 + ((parent >> 7) & 1) * 2 + (parent & 1)
    key = rows_of(line.astype(f32), N_DP * N_MP)

    weighted = (keep_ref[...] * scale).astype(bf16).astype(f32) * count_ref[0:1, :]
    part = (parent >> 1) & 3
    both = jnp.concatenate([jnp.where(part == s, weighted, 0.0) for s in range(4)], axis=0)
    high = both.astype(bf16)
    low = (both - high.astype(f32)).astype(bf16)
    total = dot_nt(key, jnp.concatenate([high, low], axis=0))
    out_ref[...] = (total[:, :128] + total[:, 128:]).astype(bf16)


def spread_kernel(in_ref, out_ref):
    total = jnp.sum(in_ref[...].astype(f32).reshape(N_DP // 2, 32, 128), axis=0).reshape(4, 8, 128)
    band, part = iota((2, 8, 128), 2) >> 5, iota((2, 8, 128), 1) >> 1
    even = jnp.concatenate([total[0:1], total[2:3]], axis=0)
    odd = jnp.concatenate([total[1:2], total[3:4]], axis=0)
    pieces = []
    for xl in range(2):
        out = jnp.zeros((2, 8, 128), f32)
        for y in range(4):
            for s in range(4):
                piece = odd if y >> 1 else even
                across, down = (32 * (y - s)) % 128, (2 * s - 4 * (y & 1) - 2 * xl) % 8
                piece = pltpu.roll(piece, across, 2) if across else piece
                piece = pltpu.roll(piece, down, 1) if down else piece
                out = jnp.where((band == y) & (part == s), piece, out)
        pieces.append(out)
    out = jnp.concatenate(pieces, axis=0)
    place = 2 * lax.axis_index("xl") + lax.axis_index("xh")
    turned = out
    for n in range(1, 4):
        turned = jnp.where(place == n, pltpu.roll(out, 32 * n, 2), turned)
    out_ref[...] = jnp.broadcast_to(turned.reshape(32, 128).astype(bf16)[None], (N_DP, 32, 128))


def finish_kernel(in_ref, level2_ref, out_hbm, level2_hbm, out_ref, sems):
    stores = [pltpu.make_async_copy(level2_ref, level2_hbm, sems.at[2])]
    stores[0].start()
    band = iota((N_DP // 2, 8, 128), 2) >> 5
    places = [(p >> 1) * 4 + (p & 1) for p in range(N_DP // 2)]
    tiles = []
    square = jnp.zeros((N_DP // 2, 8, 128), f32)
    for t in range(2):
        block = pl.ds(8 * t, 8)
        parts = []
        for n in range(4):
            source = [2 * (place + 2 * (n & 1)) + (n >> 1) for place in places]
            parts.append(jnp.concatenate([in_ref[m : m + 1, block, :] for m in source], axis=0).astype(f32))
        for y in range(4):
            tile = parts[0]
            for n in range(1, 4):
                tile = jnp.where(band == (y + n) % 4, parts[n], tile)
            tile = pltpu.roll(tile, 128 - 32 * y, 2) if y else tile
            tiles.append(tile)
            square = square + tile * tile
    scale = lax.rsqrt(jnp.sum(square, axis=2, keepdims=True) * (1.0 / D) + EPS)
    for n in range(2):
        block = pl.ds(64 * n, 64)
        for c in range(8):
            part = tiles[c][8 * n : 8 * n + 8] * scale[8 * n : 8 * n + 8]
            out_ref[block, 128 * c : 128 * (c + 1)] = part.reshape(64, 128).astype(bf16)
        stores.append(pltpu.make_async_copy(out_ref.at[block], out_hbm.at[block], sems.at[n]))
        stores[-1].start()
    for store in stores:
        store.wait()


def call(kernel, out, *args, far=(), scratch=(), spaces=(pltpu.VMEM,)):
    many = isinstance(out, tuple)
    results = tuple(pl.BlockSpec(memory_space=space) for space in spaces)
    return pl.pallas_call(
        kernel,
        out_shape=out,
        in_specs=[pl.BlockSpec(memory_space=pltpu.HBM)] * len(far)
        + [pl.BlockSpec(memory_space=pltpu.VMEM)] * len(args),
        out_specs=results if many else results[0],
        scratch_shapes=scratch,
        compiler_params=pltpu.CompilerParams(vmem_limit_bytes=48 * 1024 * 1024),
    )(*(pltpu.with_memory_space_constraint(x, pltpu.HBM) for x in far), *args)


def shape(dims, dtype):
    return jax.ShapeDtypeStruct(dims, dtype)


def exchange(x, axis):
    return lax.all_to_all(x, axis, 0, 0, tiled=True)


def body(points, point_cluster, cluster_parent):
    rows = N_DP * STRIDE
    sent = call(
        sort_kernel,
        shape((rows, 128), bf16),
        far=(point_cluster.T, points.T),
        scratch=(
            pltpu.VMEM((1, PTS), i32),
            pltpu.VMEM((FEAT, PTS), bf16),
            pltpu.VMEM((rows, 128), f32),
            pltpu.SemaphoreType.DMA((2,)),
        ),
    )
    got = exchange(sent.reshape(N_DP, STRIDE // 2, 2, 128), ("z", "xh", "core")).reshape(rows, 128)
    sums, keep, counts = call(
        sum_kernel,
        (shape((2 * N_MP, 16, 128), bf16), shape((32, 2 * GROUP), f32), shape((8, 2 * GROUP), f32)),
        got,
        far=(cluster_parent.T,),
        scratch=(
            pltpu.VMEM((1, ROWS), i32),
            pltpu.VMEM((rows, 128), f32),
            pltpu.SemaphoreType.DMA(()),
        ),
        spaces=(pltpu.VMEM,) * 3,
    )
    peers = N_DP // 2 * N_MP // 2
    level2, partial = call(
        unit_kernel,
        (shape((ROWS, D), bf16), shape((4 * peers, 128), bf16)),
        exchange(sums, ("y", "xh", "xl")),
        keep,
        counts,
        spaces=(pltpu.VMEM, pltpu.VMEM),
    )
    parts = exchange(partial.reshape(peers, 4, 128), ("z", "core", "y")).reshape(4 * peers, 128)
    parents = call(spread_kernel, shape((N_DP, 32, 128), bf16), parts)
    level3, level2 = call(
        finish_kernel,
        (shape((K3_MP, D), bf16), shape((ROWS, D), bf16)),
        exchange(parents.reshape(2 * N_DP, 16, 128), ("z", "xh", "core", "xl")),
        level2,
        scratch=(pltpu.VMEM((K3_MP, D), bf16), pltpu.SemaphoreType.DMA((3,))),
        spaces=(pltpu.HBM, pltpu.HBM),
    )
    return (level2, level3)


def solution(mesh):
    split = Mesh(mesh.devices.reshape(N_DP // 4, 2, 2, N_MP // 2, 2), ("z", "xh", "core", "y", "xl"))
    dp, mp = ("z", "xh", "core"), ("y", "xl")
    placed = (P(dp, mp), P(dp, None), P((*dp, *mp), None))
    return jax.shard_map(
        body,
        mesh=split,
        in_specs=placed,
        out_specs=(P((*dp, *mp), None), P(mp, None)),
        check_vma=False,
    )
```
